32 devices in a mesh: dp: 4 (over z), row: 2 (over x), col: 4 (over y, core).
Axes of the slice: x: 2, y: 2, z: 4, core: 2. Of those that a mesh axis runs over, the one named last changes fastest.
Arguments:
- tokens: bfloat16 [2048, 1024], P(('dp', 'col'), 'row'), may hold values from -6 to 6
- seq_lengths: int32 [4, 3], P('dp'), may hold values from 1 to 448, 512 in all within a row
- norm1_gain: float32 [1024], P('row'), may hold values from 0.1 to 1.9
- w_query: bfloat16 [1024, 1024], P('row', 'col'), may hold values from -0.1875 to 0.1875
- w_key: bfloat16 [1024, 1024], P('row', 'col'), may hold values from -0.1875 to 0.1875
- w_value: bfloat16 [1024, 1024], P('row', 'col'), may hold values from -0.1875 to 0.1875
- b_query: float32 [1024], P('col'), may hold values from -3 to 3
- b_key: float32 [1024], P('col'), may hold values from -3 to 3
- b_value: float32 [1024], P('col'), may hold values from -3 to 3
- w_out: bfloat16 [1024, 1024], P('col', 'row'), may hold values from -1.5 to 1.5
- norm2_gain: float32 [1024], P('row'), may hold values from 0.1 to 1.9
- w_gate: bfloat16 [1024, 2816], P('row', 'col'), may hold values from -0.1875 to 0.1875
- w_up: bfloat16 [1024, 2816], P('row', 'col'), may hold values from -0.1875 to 0.1875
- w_down: bfloat16 [2816, 1024], P('col', 'row'), may hold values from -0.109375 to 0.109375
- cotangent: bfloat16 [2048, 1024], P(('dp', 'col'), 'row'), may hold values from -6 to 6
Outputs:
- layer_out: bfloat16 [2048, 1024], P(('dp', 'col'), 'row')
- d_tokens: bfloat16 [2048, 1024], P(('dp', 'col'), 'row')
- d_norm1_gain: float32 [1024], P('row')
- d_w_query: float32 [1024, 1024], P('row', 'col')
- d_w_key: float32 [1024, 1024], P('row', 'col')
- d_w_value: float32 [1024, 1024], P('row', 'col')
- d_b_query: float32 [1024], P('col')
- d_b_key: float32 [1024], P('col')
- d_b_value: float32 [1024], P('col')
- d_w_out: float32 [1024, 1024], P('col', 'row')
- d_norm2_gain: float32 [1024], P('row')
- d_w_gate: float32 [1024, 2816], P('row', 'col')
- d_w_up: float32 [1024, 2816], P('row', 'col')
- d_w_down: float32 [2816, 1024], P('col', 'row')
The draws below stay inside these ranges and needn't reach their ends.
Inputs may be any that keep to these rules, and one draw needn't show every extreme that they name: `seq_lengths`: each row holds 3 lengths that sum to 512, one of them exactly 448.
All inputs are finite; a program needn't handle non-finite values.
Results may differ from the reference program's by a relative error of at most 0.035.
Values may be sent and summed in bfloat16 or wider, within the bound.
A program may use at most 128 MiB of HBM per device.

```python
import math
import jax
import jax.numpy as jnp
import numpy as np
from jax import lax

D = 1024
HEADS = 16
HEAD_DIM = 64
FF = 2816
SEQS = 3
TOK_GROUP = 512
TOKENS = 2048
LONGEST = 448
N_DP = 4


def block_levels(own_key, shape, cuts, least, top_value):
    loudness, own = 1.0, jax.random.fold_in(own_key, 6)
    for dim, parts in cuts:
        steps = jnp.exp(jax.random.uniform(jax.random.fold_in(own, dim), (parts,), jnp.float32, least / len(cuts), top_value / len(cuts)))
        loudness = loudness * jnp.repeat(steps, shape[dim] // parts).reshape([-1 if axis == dim else 1 for axis in range(len(shape))])
    return loudness


def split_up(number_of, total, reach, lean):
    weights = [(1 << 20) // math.isqrt(standing ** lean) + 1 for standing in range(2, number_of + 1)]
    spare, given = total - reach - (number_of - 1), [1] * (number_of - 1)
    while spare > 0:
        movable = [i for i in range(number_of - 1) if given[i] < reach]
        mass, left = sum([weights[i] for i in movable]), spare
        for i in movable:
            more = min(reach - given[i], max(1, left * weights[i] // mass), spare)
            given[i] = given[i] + more
            spare = spare - more
    return np.array([reach] + given)


def uneven_parts(key, amount, total, limit, slope):
    if amount == 2:
        one = jax.random.randint(key, (), max(1, total - limit), min(limit, total - 1) + 1)
        return jnp.stack([one, total - one])
    sizes = jnp.asarray(split_up(amount, total, limit, slope), jnp.int32)
    pairs = (amount - 1) // 2
    donor, receiver = sizes[1:1 + 2 * pairs:2], sizes[2:2 + 2 * pairs:2]
    slack = jnp.minimum(donor - 1, limit - receiver)
    shifted = jax.random.randint(jax.random.fold_in(key, 1), (pairs,), 0, 1 << 20) % (slack + 1)
    sizes = sizes.at[1:1 + 2 * pairs:2].set(donor - shifted).at[2:2 + 2 * pairs:2].set(receiver + shifted)
    return sizes[jax.random.permutation(jax.random.fold_in(key, 2), amount)]


def bell_draw(own_key, dims, width, limit, shards=(), held_as=jnp.bfloat16):
    factor_of = block_levels(own_key, dims, shards, -0.22, 0.18) if shards else 1.0
    values = jax.random.normal(own_key, dims, jnp.float32) * width * factor_of
    return jnp.minimum(jnp.maximum(values, -limit), limit).astype(held_as)


def setup_inputs(seed: int = 0) -> dict:
    splits = jax.random.split(jax.random.key(seed), 16)
    return {
        "tokens": bell_draw(splits[0], (TOKENS, D), 1.0, 6.0, ((0, 16), (1, 2))),
        "seq_lengths": jax.vmap(lambda own: uneven_parts(own, SEQS, TOK_GROUP, LONGEST, 2))(jax.random.split(splits[1], N_DP)).reshape((N_DP, SEQS)).astype(jnp.int32),
        "norm1_gain": jnp.clip(1.0 + 0.18 * jax.random.normal(splits[2], (D,), jnp.float32), 0.1, 1.9),
        "w_query": bell_draw(splits[3], (D, HEADS * HEAD_DIM), D ** -0.5, 0.1875, ((0, 2), (1, 4))),
        "w_key": bell_draw(splits[4], (D, HEADS * HEAD_DIM), D ** -0.5, 0.1875, ((0, 2), (1, 4))),
        "w_value": bell_draw(splits[5], (D, HEADS * HEAD_DIM), D ** -0.5, 0.1875, ((0, 2), (1, 4))),
        "b_query": bell_draw(splits[6], (HEADS * HEAD_DIM,), 0.5, 3.0, ((0, 4),), jnp.float32),
        "b_key": bell_draw(splits[7], (HEADS * HEAD_DIM,), 0.5, 3.0, ((0, 4),), jnp.float32),
        "b_value": bell_draw(splits[8], (HEADS * HEAD_DIM,), 0.5, 3.0, ((0, 4),), jnp.float32),
        "w_out": bell_draw(splits[9], (HEADS * HEAD_DIM, D), (max(2, D // 64)) ** -0.5, 1.5, ((0, 4), (1, 2))),
        "norm2_gain": jnp.clip(1.0 + 0.18 * jax.random.normal(splits[10], (D,), jnp.float32), 0.1, 1.9),
        "w_gate": bell_draw(splits[11], (D, FF), D ** -0.5, 0.1875, ((0, 2), (1, 4))),
        "w_up": bell_draw(splits[12], (D, FF), D ** -0.5, 0.1875, ((0, 2), (1, 4))),
        "w_down": bell_draw(splits[13], (FF, D), FF ** -0.5, 0.109375, ((0, 4), (1, 2))),
        "cotangent": bell_draw(splits[14], (TOKENS, D), 1.0, 6.0, ((0, 16), (1, 2))),
    }


NORM_EPS = 1e-06
ROPE_THETA = 1000000.0

@jax.custom_vjp
def low(v):
    return lax.optimization_barrier(v.astype(jnp.bfloat16)).astype(jnp.float32)

@jax.custom_vjp
def low_back(v):
    return v

def low_keep(v):
    return (low(v), None)

def low_pass(kept, grad):
    return (grad,)

def back_keep(v):
    return (v, None)

def back_low(kept, grad):
    return (low(grad),)
low.defvjp(low_keep, low_pass)
low_back.defvjp(back_keep, back_low)

def matmul_hi(left, right):
    return jnp.dot(left, right, precision=lax.Precision.HIGHEST, preferred_element_type=jnp.float32)

def rmsnorm(values, gain):
    return values * lax.rsqrt(lax.optimization_barrier(jnp.mean(values * values, axis=1, keepdims=True)) + NORM_EPS) * gain

def layout(lengths):
    seq_ends = jnp.cumsum(lengths).astype(jnp.int32)
    token_place = jnp.arange(TOK_GROUP, dtype=jnp.int32)
    seq_ids = lax.optimization_barrier(jnp.sum((token_place[:, None] >= seq_ends[None, :]).astype(jnp.int32), axis=1))
    seq_starts = seq_ends - lengths
    onehot = (seq_ids[:, None] == jnp.arange(SEQS, dtype=jnp.int32)[None, :]).astype(jnp.int32)
    position = token_place - lax.optimization_barrier(jnp.sum(onehot * seq_starts[None, :], axis=1))
    allowed = (seq_ids[:, None] == seq_ids[None, :]) & (token_place[None, :] <= token_place[:, None])
    freqs = ROPE_THETA ** (-(jnp.arange(HEAD_DIM // 2, dtype=jnp.float32) * 2.0 / HEAD_DIM))
    angles = position.astype(jnp.float32)[:, None] * freqs[None, :]
    return (jnp.cos(angles), jnp.sin(angles), allowed)

def rotate(values, rot_cos, rot_sin):
    half_dim = HEAD_DIM // 2
    first = values[..., :half_dim]
    second = values[..., half_dim:]
    cos_b = rot_cos[:, None, :]
    sin_b = rot_sin[:, None, :]
    return jnp.concatenate([first * cos_b - second * sin_b, second * cos_b + first * sin_b], axis=-1)

def attend_head(query, keys, values, allowed):
    scores = low_back(jnp.where(allowed, matmul_hi(query, keys.T) * HEAD_DIM ** (-0.5), -1000000000.0))
    probs = jax.nn.softmax(scores, axis=-1)
    return matmul_hi(low(probs), values)

def forward(params, resid, rot_cos, rot_sin, allowed):
    g_one, wq_f, wk_f, wv_f, bq_f, bk_f, bv_f, wo_f, g_two, wg_f, wu_f, wd_f = params
    normed = low(rmsnorm(resid, g_one))
    query = low_back(matmul_hi(normed, wq_f) + bq_f).reshape(TOK_GROUP, HEADS, HEAD_DIM)
    keys = low_back(matmul_hi(normed, wk_f) + bk_f).reshape(TOK_GROUP, HEADS, HEAD_DIM)
    values = low(low_back(matmul_hi(normed, wv_f) + bv_f).reshape(TOK_GROUP, HEADS, HEAD_DIM))
    q_rot = low(rotate(query, rot_cos, rot_sin))
    k_rot = low(rotate(keys, rot_cos, rot_sin))

    def per_head(triple):
        return attend_head(triple[0], triple[1], triple[2], allowed)
    stacked = lax.map(jax.checkpoint(per_head), (q_rot.transpose(1, 0, 2), k_rot.transpose(1, 0, 2), values.transpose(1, 0, 2)))
    heads = low_back(low(stacked.transpose(1, 0, 2).reshape(TOK_GROUP, HEADS * HEAD_DIM)))
    hidden_one = resid + low_back(matmul_hi(heads, wo_f))
    normed_two = low(rmsnorm(hidden_one, g_two))
    gate = low_back(matmul_hi(normed_two, wg_f))
    upper = low_back(matmul_hi(normed_two, wu_f))
    hidden = low_back(low(jax.nn.silu(gate) * upper))
    return hidden_one + low_back(matmul_hi(hidden, wd_f))

def reference(tokens, seq_lengths, norm1_gain, w_query, w_key, w_value, b_query, b_key, b_value, w_out, norm2_gain, w_gate, w_up, w_down, cotangent):
    params = tuple((p.astype(jnp.float32) for p in (norm1_gain, w_query, w_key, w_value, b_query, b_key, b_value, w_out, norm2_gain, w_gate, w_up, w_down)))
    inputs = tokens.astype(jnp.float32).reshape(N_DP, TOK_GROUP, D)
    cotangents = cotangent.astype(jnp.float32).reshape(N_DP, TOK_GROUP, D)

    def group_step(running, group_data):
        resid, lengths, cot_group = group_data
        rot_cos, rot_sin, allowed = layout(lengths)

        def forward_fn(prm, values):
            return forward(prm, values, rot_cos, rot_sin, allowed)
        result, pullback = jax.vjp(forward_fn, params, resid)
        d_params, d_input = pullback(cot_group)
        running = jax.tree.map(lambda acc, new: acc + new, running, d_params)
        return (running, (result, d_input))
    start_grads = jax.tree.map(jnp.zeros_like, params)
    grads, (results, d_inputs) = lax.scan(group_step, start_grads, (inputs, seq_lengths.astype(jnp.int32), cotangents))
    layer_out = results.reshape(TOKENS, D).astype(jnp.bfloat16)
    d_tokens = d_inputs.reshape(TOKENS, D).astype(jnp.bfloat16)
    return (layer_out, d_tokens, grads[0], grads[1], grads[2], grads[3], grads[4], grads[5], grads[6], grads[7], grads[8], grads[9], grads[10], grads[11])
```

```python
import functools

import jax
import jax.numpy as jnp
from jax import lax
from jax.experimental import pallas as pl
from jax.experimental.pallas import tpu as pltpu
from jax.sharding import PartitionSpec as P

HEAD_DIM = 64
NORM_EPS = 1e-06
ROPE_THETA = 1000000.0
MESH = pl.DeviceIdType.MESH
F32 = jnp.float32
BF16 = jnp.bfloat16


def dot_plain(left, right):
    return jnp.dot(left, right, preferred_element_type=F32)


def dot_left_t(left, right):
    return lax.dot_general(left, right, (((0,), (0,)), ((), ())), preferred_element_type=F32)


def dot_right_t(left, right):
    return lax.dot_general(left, right, (((1,), (1,)), ((), ())), preferred_element_type=F32)


class Plane:
    def __init__(self, rows, cols):
        self.row = lax.axis_index("row")
        col = lax.axis_index("col")
        self.chip, self.core = col // 2, col % 2
        self.n_row, self.n_chip = rows, cols // 2
        self.offsets = [
            (dr, dc) for dr in range(rows) for dc in range(cols // 2) if (dr, dc) != (0, 0)
        ]

    def sibling(self):
        return {"row": self.row, "col": self.chip * 2 + 1 - self.core}

    def place(self, dr, dc, sign=1):
        return (
            lax.rem(self.row + sign * dr + self.n_row, self.n_row),
            lax.rem(self.chip + sign * dc + self.n_chip, self.n_chip),
        )

    def device(self, place):
        return {"row": place[0], "col": place[1] * 2 + self.core}

    def barrier(self):
        sem = pltpu.get_barrier_semaphore()
        peers = [self.sibling()] + [self.device(self.place(*off)) for off in self.offsets]
        for peer in peers:
            pl.semaphore_signal(sem, inc=1, device_id=peer, device_id_type=MESH)
        pl.semaphore_wait(sem, len(peers))


def block_of(ref, place, core, height, width):
    top = pl.multiple_of((place[1] * 2 + core) * height, height)
    left = pl.multiple_of(place[0] * width, width)
    return ref.at[pl.ds(top, height), pl.ds(left, width)]


def remote(src, dst, send, recv, device):
    return pltpu.make_async_remote_copy(
        src_ref=src, dst_ref=dst, send_sem=send, recv_sem=recv, device_id=device, device_id_type=MESH
    )


def gather_start(plane, out, height, width, sems):
    sib_send, sib_recv, chip_send, chip_recv = sems
    here = (plane.row, plane.chip)
    own = block_of(out, here, plane.core, height, width)
    copies = []
    for k, off in enumerate(plane.offsets):
        copy = remote(own, own, chip_send.at[k], chip_recv.at[k], plane.device(plane.place(*off)))
        copy.start()
        copies.append(copy)
    last = len(plane.offsets)
    copy = remote(own, own, sib_send.at[last], sib_recv.at[last], plane.sibling())
    copy.start()
    copies.append(copy)
    return copies


def gather_end(plane, out, height, width, sems, copies):
    sib_send, sib_recv, chip_send, chip_recv = sems
    for k, off in enumerate(plane.offsets):
        block = block_of(out, plane.place(*off, sign=-1), plane.core, height, width)
        remote(block, block, chip_send.at[k], chip_recv.at[k], plane.sibling()).wait_recv()
        copy = remote(block, block, sib_send.at[k], sib_recv.at[k], plane.sibling())
        copy.start()
        copies.append(copy)
    for k, off in enumerate(plane.offsets + [(0, 0)]):
        block = block_of(out, plane.place(*off, sign=-1), 1 - plane.core, height, width)
        remote(block, block, sib_send.at[k], sib_recv.at[k], plane.sibling()).wait_recv()
    for copy in copies:
        copy.wait_send()


def gather_kernel(rows, cols, count, *refs):
    ins, outs, sems = refs[:count], refs[count : 2 * count], refs[2 * count :]
    plane = Plane(rows, cols)
    height, width = ins[0].shape
    here = (plane.row, plane.chip)
    for src, out in zip(ins, outs):
        block_of(out, here, plane.core, height, width)[...] = src[...]
    plane.barrier()
    pending = []
    for i, out in enumerate(outs):
        own_sems = [sem.at[i] for sem in sems]
        pending.append((out, own_sems, gather_start(plane, out, height, width, own_sems)))
    for out, own_sems, copies in pending:
        gather_end(plane, out, height, width, own_sems, copies)


def reduce_kernel(rows, cols, gather, part, addend, *refs):
    out, sib_buf, send_buf, recv_buf, s_send, s_recv, c_send, c_recv = refs[:8]
    plane = Plane(rows, cols)
    height, width = addend.shape
    here = (plane.row, plane.chip)
    plane.barrier()
    sib_copies = []
    for dc in reversed(range(plane.n_chip)):
        chip = plane.place(0, dc)[1]
        top = pl.multiple_of((chip * 2 + 1 - plane.core) * height, height)
        copy = remote(
            part.at[pl.ds(top, height), :],
            sib_buf.at[dc],
            s_send.at[dc],
            s_recv.at[dc],
            plane.sibling(),
        )
        copy.start()
        sib_copies.append(copy)

    def both(place, dc):
        left = pl.multiple_of(place[0] * width, width)
        own = block_of(part, place, plane.core, height, width)[...]
        return own.astype(F32) + sib_buf[dc, :, pl.ds(left, width)].astype(F32)

    copies = []
    waited = set()
    order = sorted(range(len(plane.offsets)), key=lambda k: (-plane.offsets[k][1], -plane.offsets[k][0]))
    for k in order:
        dr, dc = plane.offsets[k]
        if dc not in waited:
            waited.add(dc)
            sib_copies[plane.n_chip - 1 - dc].wait_recv()
        place = plane.place(dr, dc)
        send_buf[k] = both(place, dc).astype(BF16)
        copy = remote(
            send_buf.at[k], recv_buf.at[k], c_send.at[k], c_recv.at[k], plane.device(place)
        )
        copy.start()
        copies.append(copy)
    if 0 not in waited:
        sib_copies[plane.n_chip - 1].wait_recv()
    total = both(here, 0) + addend[...].astype(F32)
    for copy in copies:
        copy.wait_recv()
    for k in range(len(plane.offsets)):
        total = total + recv_buf[k].astype(F32)
    if gather:
        block_of(out, here, plane.core, height, width)[...] = total.astype(out.dtype)
        sems = refs[8:]
        pending = gather_start(plane, out, height, width, sems)
        gather_end(plane, out, height, width, sems, pending)
    else:
        out[...] = total.astype(out.dtype)
    for copy in copies + sib_copies:
        copy.wait_send()


def dma(*shape):
    return pltpu.SemaphoreType.DMA(shape)


def params(collective_id):
    return pltpu.CompilerParams(
        collective_id=collective_id, has_side_effects=True, vmem_limit_bytes=32 << 20
    )


VMEM = pl.BlockSpec(memory_space=pltpu.VMEM)


def plane_gather(blocks, collective_id):
    rows, cols = lax.axis_size("row"), lax.axis_size("col")
    chips = rows * cols // 2
    count = len(blocks)
    height, width = blocks[0].shape
    return pl.pallas_call(
        functools.partial(gather_kernel, rows, cols, count),
        out_shape=[jax.ShapeDtypeStruct((height * cols, width * rows), b.dtype) for b in blocks],
        in_specs=[VMEM] * count,
        out_specs=[VMEM] * count,
        scratch_shapes=[dma(count, chips), dma(count, chips), dma(count, chips), dma(count, chips)],
        compiler_params=params(collective_id),
        name=f"plane_gather_{collective_id}",
    )(*blocks)


def plane_reduce(part, addend, gather, collective_id):
    rows, cols = lax.axis_size("row"), lax.axis_size("col")
    chips = rows * cols // 2
    height, width = addend.shape
    scratch = [
        pltpu.VMEM((cols // 2, height, width * rows), BF16),
        pltpu.VMEM((chips - 1, height, width), BF16),
        pltpu.VMEM((chips - 1, height, width), BF16),
        dma(cols // 2),
        dma(cols // 2),
        dma(chips - 1),
        dma(chips - 1),
    ]
    if gather:
        scratch += [dma(chips), dma(chips), dma(chips), dma(chips)]
        shape = (height * cols, width * rows)
    else:
        shape = (height, width)
    return pl.pallas_call(
        functools.partial(reduce_kernel, rows, cols, gather),
        out_shape=jax.ShapeDtypeStruct(shape, BF16),
        in_specs=[VMEM] * 2,
        out_specs=VMEM,
        scratch_shapes=scratch,
        compiler_params=params(collective_id),
        name=f"plane_reduce_{collective_id}",
    )(part, addend)


def swap_rows(value):
    return lax.ppermute(value, "row", [(0, 1), (1, 0)])


def half_of(value, index, axis):
    size = value.shape[axis] // 2
    return lax.dynamic_slice_in_dim(value, index * size, size, axis)


def in_order(row, own, other, axis):
    return jnp.where(
        row == 0,
        jnp.concatenate([own, other], axis),
        jnp.concatenate([other, own], axis),
    )


def whole_of_half(weight, row, cut, join):
    other = swap_rows(half_of(weight, 1 - row, cut))
    return in_order(row, half_of(weight, row, cut), other, join)


def unit_of(values):
    inverse = lax.rsqrt(jnp.mean(values * values, axis=1, keepdims=True) + NORM_EPS)
    return values * inverse, inverse


def norm_back(d_normed, gain, unit, inverse):
    scaled = d_normed * gain
    inner = jnp.sum(scaled * unit, axis=1, keepdims=True)
    return inverse * (scaled - unit * (inner / unit.shape[1]))


def layout(lengths, group_len):
    seq_ends = jnp.cumsum(lengths)
    token_place = jnp.arange(group_len, dtype=jnp.int32)
    seq_ids = jnp.sum((token_place[:, None] >= seq_ends[None, :]).astype(jnp.int32), axis=1)
    seq_starts = seq_ends - lengths
    onehot = (seq_ids[:, None] == jnp.arange(lengths.shape[0], dtype=jnp.int32)[None, :]).astype(
        jnp.int32
    )
    position = token_place - jnp.sum(onehot * seq_starts[None, :], axis=1)
    allowed = (seq_ids[:, None] == seq_ids[None, :]) & (
        token_place[None, :] <= token_place[:, None]
    )
    freqs = ROPE_THETA ** (-(jnp.arange(HEAD_DIM // 2, dtype=F32) * 2.0 / HEAD_DIM))
    angles = position.astype(F32)[:, None] * freqs[None, :]
    return (jnp.cos(angles), jnp.sin(angles), allowed)


def rotate(values, rot_cos, rot_sin):
    half_dim = HEAD_DIM // 2
    first, second = values[..., :half_dim], values[..., half_dim:]
    return jnp.concatenate(
        [first * rot_cos - second * rot_sin, second * rot_cos + first * rot_sin], axis=-1
    )


def to_heads(values):
    return [values[:, i : i + HEAD_DIM] for i in range(0, values.shape[1], HEAD_DIM)]


def group_sum(grad, row, axis):
    count = lax.axis_size("dp")
    place = lax.axis_index("dp")
    ring = [(i, (i + 1) % count) for i in range(count)]
    if axis == 0:
        pieces = grad.reshape(2, count, grad.shape[0] // (2 * count), grad.shape[1])
    else:
        pieces = grad.reshape(count, grad.shape[0] // count, 2, grad.shape[1] // 2)
        pieces = pieces.transpose(2, 0, 1, 3)

    def chunk(index):
        return lax.dynamic_index_in_dim(pieces, index % count, 1, keepdims=False)

    held = chunk(place - 1 + count).astype(BF16)
    for step in range(count - 1):
        came = lax.ppermute(held, "dp", ring)
        held = (came.astype(F32) + chunk(place - step - 2 + 2 * count)).astype(BF16)
    own = lax.dynamic_index_in_dim(held, row, 0, keepdims=False)
    other = swap_rows(lax.dynamic_index_in_dim(held, 1 - row, 0, keepdims=False))
    if axis == 0:
        held = in_order(row, own, other, 1)[None]
    else:
        held = in_order(row, own[None], other[None], 0)
    whole = jnp.zeros((held.shape[0], count) + held.shape[1:], F32)
    for step in range(count):
        whole = lax.dynamic_update_index_in_dim(
            whole, held.astype(F32), (place - step + count) % count, 1
        )
        if step < count - 1:
            held = lax.ppermute(held, "dp", ring)
    return whole.reshape(-1, whole.shape[-1])


def on_device(
    tokens,
    seq_lengths,
    norm1_gain,
    w_query,
    w_key,
    w_value,
    b_query,
    b_key,
    b_value,
    w_out,
    norm2_gain,
    w_gate,
    w_up,
    w_down,
    cotangent,
):
    height, width = tokens.shape
    row, col = lax.axis_index("row"), lax.axis_index("col")
    rows, cols = lax.axis_size("row"), lax.axis_size("col")
    group_len = height * cols
    scale = HEAD_DIM ** (-0.5)

    def own_block(full):
        return lax.dynamic_slice(full, (col * height, row * width), (height, width))

    def joined_half(parts):
        return jnp.concatenate([half_of(part, row, 0) for part in parts])

    w_qkv_own = jnp.concatenate([half_of(w, row, 1) for w in (w_query, w_key, w_value)], 1)
    w_qkv_other = swap_rows(
        jnp.concatenate([half_of(w, 1 - row, 1) for w in (w_query, w_key, w_value)], 1)
    )
    w_qkv = in_order(row, w_qkv_own, w_qkv_other, 0)
    gains = jnp.stack([norm1_gain, norm2_gain])
    gains = in_order(row, gains, swap_rows(gains), 1)
    w_o = whole_of_half(w_out, row, 0, 1)
    w_g = whole_of_half(w_gate, row, 1, 0)
    w_u = whole_of_half(w_up, row, 1, 0)
    w_d = whole_of_half(w_down, row, 0, 1)

    token_full, cot_full = plane_gather([tokens, cotangent], 0)
    resid = token_full.astype(F32)
    unit_one, inverse_one = unit_of(resid)
    normed_one = (unit_one * gains[0:1]).astype(BF16)
    qkv = dot_plain(normed_one, w_qkv) + joined_half((b_query, b_key, b_value))
    own_cols = qkv.shape[1] // 3
    rot_cos, rot_sin, allowed = layout(seq_lengths[0], group_len)
    q_heads = [rotate(h, rot_cos, rot_sin).astype(BF16) for h in to_heads(qkv[:, :own_cols])]
    k_heads = [
        rotate(h, rot_cos, rot_sin).astype(BF16) for h in to_heads(qkv[:, own_cols : 2 * own_cols])
    ]
    v_heads = [h.astype(BF16) for h in to_heads(qkv[:, 2 * own_cols :])]
    head_outs, head_probs = [], []
    for query, keys, values in zip(q_heads, k_heads, v_heads):
        scores = jnp.where(allowed, dot_right_t(query, keys) * scale, -1000000000.0)
        expo = jnp.exp(scores - jnp.max(scores, axis=-1, keepdims=True))
        probs = expo / jnp.sum(expo, axis=-1, keepdims=True)
        head_probs.append(probs)
        head_outs.append(dot_plain(probs.astype(BF16), values).astype(BF16))
    heads = jnp.concatenate(head_outs, 1)
    h1_full = plane_reduce(dot_plain(heads, w_o).astype(BF16), tokens, True, 1)
    unit_two, inverse_two = unit_of(h1_full.astype(F32))
    normed_two = (unit_two * gains[1:2]).astype(BF16)
    gate, upper = dot_plain(normed_two, w_g), dot_plain(normed_two, w_u)
    sigmoid_gate = jax.nn.sigmoid(gate)
    silu_gate = gate * sigmoid_gate
    hidden = (silu_gate * upper).astype(BF16)
    d_hidden = dot_right_t(cot_full, w_d).astype(BF16).astype(F32)
    d_gate = (d_hidden * upper * sigmoid_gate * (1.0 + gate * (1.0 - sigmoid_gate))).astype(BF16)
    d_upper = (d_hidden * silu_gate).astype(BF16)
    part = (dot_right_t(d_gate, w_g) + dot_right_t(d_upper, w_u)).astype(BF16)
    no_block = jnp.zeros((height, width), BF16)
    d_normed_two = plane_reduce(part, no_block, True, 2).astype(F32)
    d_h1 = norm_back(d_normed_two, gains[1:2], unit_two, inverse_two) + cot_full.astype(F32)
    d_gain_two = jnp.sum(own_block(d_normed_two) * own_block(unit_two), axis=0)

    d_w_gate = group_sum(dot_left_t(normed_two, d_gate), row, 0)
    d_w_up = group_sum(dot_left_t(normed_two, d_upper), row, 0)
    d_w_down = group_sum(dot_left_t(hidden, cot_full), row, 1)
    layer_out = plane_reduce(dot_plain(hidden, w_d).astype(BF16), own_block(h1_full), False, 4)

    d_branch = d_h1.astype(BF16)
    d_w_out = group_sum(dot_left_t(heads, d_branch), row, 1)
    d_heads = dot_right_t(d_branch, w_o).astype(BF16)
    d_q, d_k, d_v = [], [], []
    for query, keys, values, probs, d_out in zip(
        q_heads, k_heads, v_heads, head_probs, to_heads(d_heads)
    ):
        d_v.append(dot_left_t(probs.astype(BF16), d_out))
        d_probs = dot_right_t(d_out, values)
        d_scores = (
            probs * (d_probs - jnp.sum(probs * d_probs, axis=-1, keepdims=True))
        ).astype(BF16)
        d_q.append(rotate(dot_plain(d_scores, keys) * scale, rot_cos, -rot_sin))
        d_k.append(rotate(dot_left_t(d_scores, query) * scale, rot_cos, -rot_sin))
    d_qkv = jnp.concatenate(d_q + d_k + d_v, 1).astype(BF16)
    part = dot_right_t(d_qkv, w_qkv).astype(BF16)
    d_normed_one = plane_reduce(part, no_block, True, 3).astype(F32)
    d_w = []
    for i in range(3):
        d_w.append(
            group_sum(dot_left_t(normed_one, d_qkv[:, i * own_cols : (i + 1) * own_cols]), row, 0)
        )
    d_tokens = (norm_back(d_normed_one, gains[0:1], unit_one, inverse_one) + d_h1).astype(BF16)
    d_tokens = own_block(d_tokens)
    d_gain_one = jnp.sum(own_block(d_normed_one) * own_block(unit_one), axis=0)
    d_bias = jnp.sum(d_qkv.astype(F32), axis=0).reshape(3, own_cols)

    gain_slots = jnp.zeros((2, rows, width), F32)
    gain_slots = lax.dynamic_update_slice(
        gain_slots, jnp.stack([d_gain_one, d_gain_two])[:, None], (0, row, 0)
    )
    bias_slots = jnp.zeros((3, cols, rows * own_cols), F32)
    bias_slots = lax.dynamic_update_slice(bias_slots, d_bias[:, None], (0, col, row * own_cols))
    small = jnp.concatenate([gain_slots.reshape(-1), bias_slots.reshape(-1)])
    small = lax.psum(small, ("dp", "row", "col"))
    gain_sum = small[: gain_slots.size].reshape(gain_slots.shape)
    bias_sum = small[gain_slots.size :].reshape(bias_slots.shape)
    gain_sum = lax.dynamic_index_in_dim(gain_sum, row, 1, keepdims=False)
    bias_sum = lax.dynamic_index_in_dim(bias_sum, col, 1, keepdims=False)
    return (
        layer_out,
        d_tokens,
        gain_sum[0],
        d_w[0],
        d_w[1],
        d_w[2],
        bias_sum[0],
        bias_sum[1],
        bias_sum[2],
        d_w_out,
        gain_sum[1],
        d_w_gate,
        d_w_up,
        d_w_down,
    )


def solution(mesh):
    block = P(("dp", "col"), "row")
    down, across = P("row", "col"), P("col", "row")
    return jax.shard_map(
        on_device,
        mesh=mesh,
        in_specs=(
            block,
            P("dp", None),
            P("row"),
            down,
            down,
            down,
            P("col"),
            P("col"),
            P("col"),
            across,
            P("row"),
            down,
            down,
            across,
            block,
        ),
        out_specs=(
            block,
            block,
            P("row"),
            down,
            down,
            down,
            P("col"),
            P("col"),
            P("col"),
            across,
            P("row"),
            down,
            down,
            across,
        ),
        check_vma=False,
    )
```

```python
import functools

import jax
import jax.numpy as jnp
from jax import lax
from jax.experimental import pallas as pl
from jax.experimental.pallas import tpu as pltpu
from jax.sharding import PartitionSpec as P

HEAD_DIM = 64
NORM_EPS = 1e-06
ROPE_THETA = 1000000.0
MESH = pl.DeviceIdType.MESH
F32 = jnp.float32
BF16 = jnp.bfloat16


def dot_plain(left, right):
    return jnp.dot(left, right, preferred_element_type=F32)


def dot_left_t(left, right):
    return lax.dot_general(left, right, (((0,), (0,)), ((), ())), preferred_element_type=F32)


def dot_right_t(left, right):
    return lax.dot_general(left, right, (((1,), (1,)), ((), ())), preferred_element_type=F32)


class Plane:
    def __init__(self, rows, cols):
        self.row = lax.axis_index("row")
        col = lax.axis_index("col")
        self.chip, self.core = col // 2, col % 2
        self.n_row, self.n_chip = rows, cols // 2
        self.offsets = [
            (dr, dc) for dr in range(rows) for dc in range(cols // 2) if (dr, dc) != (0, 0)
        ]

    def sibling(self):
        return {"row": self.row, "col": self.chip * 2 + 1 - self.core}

    def place(self, dr, dc, sign=1):
        return (
            lax.rem(self.row + sign * dr + self.n_row, self.n_row),
            lax.rem(self.chip + sign * dc + self.n_chip, self.n_chip),
        )

    def device(self, place):
        return {"row": place[0], "col": place[1] * 2 + self.core}

    def barrier(self, extra=()):
        sem = pltpu.get_barrier_semaphore()
        peers = [self.sibling()] + [self.device(self.place(*off)) for off in self.offsets]
        peers += list(extra)
        for peer in peers:
            pl.semaphore_signal(sem, inc=1, device_id=peer, device_id_type=MESH)
        pl.semaphore_wait(sem, len(peers))


def block_of(ref, place, core, height, width):
    top = pl.multiple_of((place[1] * 2 + core) * height, height)
    left = pl.multiple_of(place[0] * width, width)
    return ref.at[pl.ds(top, height), pl.ds(left, width)]


def remote(src, dst, send, recv, device):
    return pltpu.make_async_remote_copy(
        src_ref=src, dst_ref=dst, send_sem=send, recv_sem=recv, device_id=device, device_id_type=MESH
    )


def gather_start(plane, out, height, width, sems):
    sib_send, sib_recv, chip_send, chip_recv = sems
    here = (plane.row, plane.chip)
    own = block_of(out, here, plane.core, height, width)
    copies = []
    for k, off in enumerate(plane.offsets):
        copy = remote(own, own, chip_send.at[k], chip_recv.at[k], plane.device(plane.place(*off)))
        copy.start()
        copies.append(copy)
    last = len(plane.offsets)
    copy = remote(own, own, sib_send.at[last], sib_recv.at[last], plane.sibling())
    copy.start()
    copies.append(copy)
    return copies


def gather_end(plane, out, height, width, sems, copies):
    sib_send, sib_recv, chip_send, chip_recv = sems
    for k, off in enumerate(plane.offsets):
        block = block_of(out, plane.place(*off, sign=-1), plane.core, height, width)
        yield
        remote(block, block, chip_send.at[k], chip_recv.at[k], plane.sibling()).wait_recv()
        copy = remote(block, block, sib_send.at[k], sib_recv.at[k], plane.sibling())
        copy.start()
        copies.append(copy)
    for k, off in enumerate(plane.offsets + [(0, 0)]):
        block = block_of(out, plane.place(*off, sign=-1), 1 - plane.core, height, width)
        yield
        remote(block, block, sib_send.at[k], sib_recv.at[k], plane.sibling()).wait_recv()
    for copy in copies:
        copy.wait_send()


def run_all(*steps):
    steps = list(steps)
    while steps:
        for step in list(steps):
            try:
                next(step)
            except StopIteration:
                steps.remove(step)


def gather_kernel(rows, cols, count, *refs):
    ins, outs, sems = refs[:count], refs[count : 2 * count], refs[2 * count :]
    plane = Plane(rows, cols)
    height, width = ins[0].shape
    here = (plane.row, plane.chip)
    for src, out in zip(ins, outs):
        block_of(out, here, plane.core, height, width)[...] = src[...]
    plane.barrier()
    pending = []
    for i, out in enumerate(outs):
        own_sems = [sem.at[i] for sem in sems]
        pending.append((out, own_sems, gather_start(plane, out, height, width, own_sems)))
    run_all(*[gather_end(plane, out, height, width, own, copies) for out, own, copies in pending])


def reduce_steps(plane, part, addend, out, scratch):
    sib_buf, send_buf, recv_buf, s_send, s_recv, c_send, c_recv = scratch[:7]
    sems = scratch[7:]
    height, width = send_buf.shape[1:]
    here = (plane.row, plane.chip)
    sib_copies = []
    for dc in reversed(range(plane.n_chip)):
        chip = plane.place(0, dc)[1]
        top = pl.multiple_of((chip * 2 + 1 - plane.core) * height, height)
        copy = remote(
            part.at[pl.ds(top, height), :],
            sib_buf.at[dc],
            s_send.at[dc],
            s_recv.at[dc],
            plane.sibling(),
        )
        copy.start()
        sib_copies.append(copy)

    def both(place, dc):
        left = pl.multiple_of(place[0] * width, width)
        own = block_of(part, place, plane.core, height, width)[...]
        return own.astype(F32) + sib_buf[dc, :, pl.ds(left, width)].astype(F32)

    copies = []
    waited = set()
    order = sorted(range(len(plane.offsets)), key=lambda k: (-plane.offsets[k][1], -plane.offsets[k][0]))
    for k in order:
        dr, dc = plane.offsets[k]
        if dc not in waited:
            waited.add(dc)
            yield
            sib_copies[plane.n_chip - 1 - dc].wait_recv()
        place = plane.place(dr, dc)
        send_buf[k] = both(place, dc).astype(BF16)
        copy = remote(
            send_buf.at[k], recv_buf.at[k], c_send.at[k], c_recv.at[k], plane.device(place)
        )
        copy.start()
        copies.append(copy)
    if 0 not in waited:
        sib_copies[plane.n_chip - 1].wait_recv()
    total = both(here, 0)
    if addend is not None:
        total = total + addend[...].astype(F32)
    for copy in copies:
        yield
        copy.wait_recv()
    for k in range(len(plane.offsets)):
        total = total + recv_buf[k].astype(F32)
    if sems:
        block_of(out, here, plane.core, height, width)[...] = total.astype(out.dtype)
        pending = gather_start(plane, out, height, width, sems)
        yield from gather_end(plane, out, height, width, sems, pending)
    else:
        out[...] = total.astype(out.dtype)
    for copy in copies + sib_copies:
        copy.wait_send()


def reduce_kernel(rows, cols, part, addend, out, *scratch):
    plane = Plane(rows, cols)
    plane.barrier()
    run_all(reduce_steps(plane, part, addend, out, scratch))


class Ring:
    def __init__(self, count):
        self.count = count
        self.place = lax.axis_index("dp")
        self.next = {"dp": self.at(1)}

    def at(self, offset):
        return lax.rem(self.place + offset + 2 * self.count, self.count)


def ring_sum_steps(ring, pieces, out, recv, send_sem, recv_sem):
    copies = []
    for step in range(ring.count - 1):
        if step == 0:
            src = pieces.at[:, ring.at(-1)]
        else:
            src = recv.at[step - 1]
        copy = remote(src, recv.at[step], send_sem.at[step], recv_sem.at[step], ring.next)
        copy.start()
        copies.append(copy)
        yield
        copy.wait_recv()
        total = recv[step].astype(F32) + pieces[:, ring.at(-step - 2)].astype(F32)
        if step < ring.count - 2:
            recv[step] = total.astype(BF16)
        else:
            out[...] = total.astype(BF16)
    for copy in copies:
        copy.wait_send()


def ring_gather_steps(ring, plane, chunk, out, row_sems, send_sem, recv_sem):
    swap = remote(
        chunk.at[1 - plane.row],
        out.at[ring.place, plane.row],
        row_sems.at[0],
        row_sems.at[1],
        plane.device((1 - plane.row, plane.chip)),
    )
    swap.start()
    out[ring.place, plane.row] = chunk[plane.row]
    yield
    landed = out.at[ring.place, 1 - plane.row]
    remote(landed, landed, row_sems.at[0], row_sems.at[1], ring.next).wait_recv()
    copies = [swap]
    for step in range(ring.count - 1):
        src = out.at[ring.at(-step)]
        copy = remote(src, src, send_sem.at[step], recv_sem.at[step], ring.next)
        copy.start()
        copies.append(copy)
        yield
        came = out.at[ring.at(-step - 1)]
        remote(came, came, send_sem.at[step], recv_sem.at[step], ring.next).wait_recv()
    for copy in copies:
        copy.wait_send()


def mlp_kernel(rows, cols, count, pieces_count, *refs):
    part, pieces = refs[0], refs[1 : 1 + pieces_count]
    refs = refs[1 + pieces_count :]
    out, chunks = refs[0], refs[1 : 1 + pieces_count]
    refs = refs[1 + pieces_count :]
    recvs, refs = refs[:pieces_count], refs[pieces_count:]
    ring_send, ring_recv = refs[:2]
    plane, ring = Plane(rows, cols), Ring(count)
    plane.barrier([ring.next, {"dp": ring.at(-1)}])
    run_all(
        reduce_steps(plane, part, None, out, refs[2:]),
        *[
            ring_sum_steps(ring, piece, chunk, recv, ring_send.at[i], ring_recv.at[i])
            for i, (piece, chunk, recv) in enumerate(zip(pieces, chunks, recvs))
        ],
    )


def last_kernel(rows, cols, count, n_mlp, n_att, *refs):
    refs = list(refs)

    def take(number):
        taken = refs[:number]
        del refs[:number]
        return taken

    part, part_out, h1_block, unit, small = take(5)
    mlp_chunks, pieces = take(n_mlp), take(n_att)
    d_normed, layer_out, small_out = take(3)
    mlp_outs, att_outs = take(n_mlp), take(n_att)
    recvs, chunks = take(n_att), take(n_att)
    small_buf, small_send, small_recv, small_row = take(4)
    row_sems, gather_send, gather_recv, ring_send, ring_recv = take(5)
    normed_scratch, out_scratch = take(11), take(7)
    plane, ring = Plane(rows, cols), Ring(count)
    others = [{"dp": ring.at(i)} for i in range(1, count)]
    plane.barrier(others)
    width = h1_block.shape[1]

    def attention(i):
        yield from ring_sum_steps(
            ring, pieces[i], chunks[i], recvs[i], ring_send.at[i], ring_recv.at[i]
        )
        k = n_mlp + i
        yield from ring_gather_steps(
            ring, plane, chunks[i], att_outs[i], row_sems.at[k], gather_send.at[k], gather_recv.at[k]
        )

    def normed():
        yield from reduce_steps(plane, part, None, d_normed, normed_scratch)
        left = pl.multiple_of(plane.row * width, width)
        gain = jnp.sum(d_normed[:, pl.ds(left, width)].astype(F32) * unit[...], axis=0, keepdims=True)
        first = lax.broadcasted_iota(jnp.int32, small.shape, 0) == 0
        small_buf[0] = jnp.where(first, gain, small[...])
        copies = []
        for i, other in enumerate(others):
            copy = remote(
                small_buf.at[0], small_buf.at[i + 1], small_send.at[i], small_recv.at[i], other
            )
            copy.start()
            copies.append(copy)
        for copy in copies:
            yield
            copy.wait()
        total = small_buf[0]
        for i in range(1, count):
            total = total + small_buf[i]
        small_out[plane.row] = total
        here = small_out.at[plane.row]
        pair = plane.device((1 - plane.row, plane.chip))
        copy = remote(here, here, small_row.at[0], small_row.at[1], pair)
        copy.start()
        yield
        there = small_out.at[1 - plane.row]
        remote(there, there, small_row.at[0], small_row.at[1], pair).wait_recv()
        copy.wait_send()

    gathers = [
        ring_gather_steps(
            ring, plane, mlp_chunks[i], mlp_outs[i], row_sems.at[i], gather_send.at[i], gather_recv.at[i]
        )
        for i in range(n_mlp)
    ]
    run_all(
        *[attention(i) for i in range(n_att)],
        *gathers,
        normed(),
        reduce_steps(plane, part_out, h1_block, layer_out, out_scratch),
    )


def dma(*shape):
    return pltpu.SemaphoreType.DMA(shape)


def params(collective_id):
    return pltpu.CompilerParams(
        collective_id=collective_id, has_side_effects=True, vmem_limit_bytes=32 << 20
    )


VMEM = pl.BlockSpec(memory_space=pltpu.VMEM)


def plane_gather(blocks, collective_id):
    rows, cols = lax.axis_size("row"), lax.axis_size("col")
    chips = rows * cols // 2
    count = len(blocks)
    height, width = blocks[0].shape
    return pl.pallas_call(
        functools.partial(gather_kernel, rows, cols, count),
        out_shape=[jax.ShapeDtypeStruct((height * cols, width * rows), b.dtype) for b in blocks],
        in_specs=[VMEM] * count,
        out_specs=[VMEM] * count,
        scratch_shapes=[dma(count, chips), dma(count, chips), dma(count, chips), dma(count, chips)],
        compiler_params=params(collective_id),
        name=f"plane_gather_{collective_id}",
    )(*blocks)


def reduce_scratch(rows, cols, height, width, gather):
    chips = rows * cols // 2
    scratch = [
        pltpu.VMEM((cols // 2, height, width * rows), BF16),
        pltpu.VMEM((chips - 1, height, width), BF16),
        pltpu.VMEM((chips - 1, height, width), BF16),
        dma(cols // 2),
        dma(cols // 2),
        dma(chips - 1),
        dma(chips - 1),
    ]
    if gather:
        scratch += [dma(chips), dma(chips), dma(chips), dma(chips)]
    return scratch


def call(kernel, ins, outs, scratch, collective_id, name):
    return pl.pallas_call(
        kernel,
        out_shape=outs,
        in_specs=[VMEM] * len(ins),
        out_specs=[VMEM] * len(outs),
        scratch_shapes=scratch,
        compiler_params=params(collective_id),
        name=name,
    )(*ins)


def shape(dims, dtype=BF16):
    return jax.ShapeDtypeStruct(tuple(dims), dtype)


def plane_reduce(part, addend):
    rows, cols = lax.axis_size("row"), lax.axis_size("col")
    height, width = addend.shape
    return call(
        functools.partial(reduce_kernel, rows, cols),
        [part, addend],
        [shape(part.shape)],
        reduce_scratch(rows, cols, height, width, True),
        1,
        "out_projection_reduce",
    )[0]


def mlp_back_reduce(part, pieces):
    rows, cols, count = lax.axis_size("row"), lax.axis_size("col"), lax.axis_size("dp")
    height, width = part.shape[0] // cols, part.shape[1] // rows
    chunks = [(p.shape[0],) + p.shape[2:] for p in pieces]
    scratch = [pltpu.VMEM((count - 1,) + c, BF16) for c in chunks]
    scratch += [dma(len(pieces), count - 1), dma(len(pieces), count - 1)]
    scratch += reduce_scratch(rows, cols, height, width, True)
    outs = call(
        functools.partial(mlp_kernel, rows, cols, count, len(pieces)),
        [part] + pieces,
        [shape(part.shape)] + [shape(c) for c in chunks],
        scratch,
        2,
        "mlp_back_reduce",
    )
    return outs[0], list(outs[1:])


def last_exchange(part, part_out, h1_block, unit, small, mlp_chunks, pieces):
    rows, cols, count = lax.axis_size("row"), lax.axis_size("col"), lax.axis_size("dp")
    height, width = h1_block.shape
    n_mlp, n_att = len(mlp_chunks), len(pieces)
    chunks = [(p.shape[0],) + p.shape[2:] for p in pieces]
    outs = [shape(part.shape), shape(h1_block.shape), shape((rows,) + small.shape, F32)]
    outs += [shape((count,) + c.shape) for c in mlp_chunks]
    outs += [shape((count,) + c) for c in chunks]
    scratch = [pltpu.VMEM((count - 1,) + c, BF16) for c in chunks]
    scratch += [pltpu.VMEM(c, BF16) for c in chunks]
    scratch += [pltpu.VMEM((count,) + small.shape, F32), dma(count - 1), dma(count - 1), dma(2)]
    scratch += [dma(n_mlp + n_att, 2), dma(n_mlp + n_att, count - 1), dma(n_mlp + n_att, count - 1)]
    scratch += [dma(n_att, count - 1), dma(n_att, count - 1)]
    scratch += reduce_scratch(rows, cols, height, width, True)
    scratch += reduce_scratch(rows, cols, height, width, False)
    outs = call(
        functools.partial(last_kernel, rows, cols, count, n_mlp, n_att),
        [part, part_out, h1_block, unit, small] + mlp_chunks + pieces,
        outs,
        scratch,
        3,
        "last_exchange",
    )
    return outs[0], outs[1], outs[2], outs[3:]


def swap_rows(value):
    return lax.ppermute(value, "row", [(0, 1), (1, 0)])


def half_of(value, index, axis):
    size = value.shape[axis] // 2
    return lax.dynamic_slice_in_dim(value, index * size, size, axis)


def in_order(row, own, other, axis):
    return jnp.where(
        row == 0,
        jnp.concatenate([own, other], axis),
        jnp.concatenate([other, own], axis),
    )


def whole_of_half(weight, row, cut, join):
    other = swap_rows(half_of(weight, 1 - row, cut))
    return in_order(row, half_of(weight, row, cut), other, join)


def unit_of(values):
    inverse = lax.rsqrt(jnp.mean(values * values, axis=1, keepdims=True) + NORM_EPS)
    return values * inverse, inverse


def norm_back(d_normed, gain, unit, inverse):
    scaled = d_normed * gain
    inner = jnp.sum(scaled * unit, axis=1, keepdims=True)
    return inverse * (scaled - unit * (inner / unit.shape[1]))


def layout(lengths, group_len):
    seq_ends = jnp.cumsum(lengths)
    token_place = jnp.arange(group_len, dtype=jnp.int32)
    seq_ids = jnp.sum((token_place[:, None] >= seq_ends[None, :]).astype(jnp.int32), axis=1)
    seq_starts = seq_ends - lengths
    onehot = (seq_ids[:, None] == jnp.arange(lengths.shape[0], dtype=jnp.int32)[None, :]).astype(
        jnp.int32
    )
    position = token_place - jnp.sum(onehot * seq_starts[None, :], axis=1)
    allowed = (seq_ids[:, None] == seq_ids[None, :]) & (
        token_place[None, :] <= token_place[:, None]
    )
    freqs = ROPE_THETA ** (-(jnp.arange(HEAD_DIM // 2, dtype=F32) * 2.0 / HEAD_DIM))
    angles = position.astype(F32)[:, None] * freqs[None, :]
    return (jnp.cos(angles), jnp.sin(angles), allowed)


def rotate(values, rot_cos, rot_sin):
    half_dim = HEAD_DIM // 2
    first, second = values[..., :half_dim], values[..., half_dim:]
    return jnp.concatenate(
        [first * rot_cos - second * rot_sin, second * rot_cos + first * rot_sin], axis=-1
    )


def to_heads(values):
    return [values[:, i : i + HEAD_DIM] for i in range(0, values.shape[1], HEAD_DIM)]


def in_chunks(grad):
    count = lax.axis_size("dp")
    grad = grad.astype(BF16)
    return grad.reshape(2, count, grad.shape[0] // (2 * count), grad.shape[1])


def from_chunks(summed):
    return summed.transpose(0, 2, 1, 3).reshape(-1, 2 * summed.shape[3]).astype(F32)


def on_device(
    tokens,
    seq_lengths,
    norm1_gain,
    w_query,
    w_key,
    w_value,
    b_query,
    b_key,
    b_value,
    w_out,
    norm2_gain,
    w_gate,
    w_up,
    w_down,
    cotangent,
):
    height, width = tokens.shape
    row, col = lax.axis_index("row"), lax.axis_index("col")
    rows, cols = lax.axis_size("row"), lax.axis_size("col")
    group_len = height * cols
    scale = HEAD_DIM ** (-0.5)

    def own_block(full):
        return lax.dynamic_slice(full, (col * height, row * width), (height, width))

    def joined_half(parts):
        return jnp.concatenate([half_of(part, row, 0) for part in parts])

    w_qkv_own = jnp.concatenate([half_of(w, row, 1) for w in (w_query, w_key, w_value)], 1)
    w_qkv_other = swap_rows(
        jnp.concatenate([half_of(w, 1 - row, 1) for w in (w_query, w_key, w_value)], 1)
    )
    w_qkv = in_order(row, w_qkv_own, w_qkv_other, 0)
    gains = jnp.stack([norm1_gain, norm2_gain])
    gains = in_order(row, gains, swap_rows(gains), 1)
    w_o = whole_of_half(w_out, row, 0, 1)
    w_g = whole_of_half(w_gate, row, 1, 0)
    w_u = whole_of_half(w_up, row, 1, 0)
    w_d = whole_of_half(w_down, row, 0, 1)

    token_full, cot_full = plane_gather([tokens, cotangent], 0)
    resid = token_full.astype(F32)
    unit_one, inverse_one = unit_of(resid)
    normed_one = (unit_one * gains[0:1]).astype(BF16)
    qkv = dot_plain(normed_one, w_qkv) + joined_half((b_query, b_key, b_value))
    own_cols = qkv.shape[1] // 3
    rot_cos, rot_sin, allowed = layout(seq_lengths[0], group_len)
    q_heads = [rotate(h, rot_cos, rot_sin).astype(BF16) for h in to_heads(qkv[:, :own_cols])]
    k_heads = [
        rotate(h, rot_cos, rot_sin).astype(BF16) for h in to_heads(qkv[:, own_cols : 2 * own_cols])
    ]
    v_heads = [h.astype(BF16) for h in to_heads(qkv[:, 2 * own_cols :])]
    head_outs, head_probs = [], []
    for query, keys, values in zip(q_heads, k_heads, v_heads):
        scores = jnp.where(allowed, dot_right_t(query, keys) * scale, -1000000000.0)
        expo = jnp.exp(scores - jnp.max(scores, axis=-1, keepdims=True))
        probs = expo / jnp.sum(expo, axis=-1, keepdims=True)
        head_probs.append(probs)
        head_outs.append(dot_plain(probs.astype(BF16), values).astype(BF16))
    heads = jnp.concatenate(head_outs, 1)
    h1_full = plane_reduce(dot_plain(heads, w_o).astype(BF16), tokens)
    unit_two, inverse_two = unit_of(h1_full.astype(F32))
    normed_two = (unit_two * gains[1:2]).astype(BF16)
    gate, upper = dot_plain(normed_two, w_g), dot_plain(normed_two, w_u)
    sigmoid_gate = jax.nn.sigmoid(gate)
    silu_gate = gate * sigmoid_gate
    hidden = (silu_gate * upper).astype(BF16)
    d_hidden = dot_right_t(cot_full, w_d).astype(BF16).astype(F32)
    d_gate = (d_hidden * upper * sigmoid_gate * (1.0 + gate * (1.0 - sigmoid_gate))).astype(BF16)
    d_upper = (d_hidden * silu_gate).astype(BF16)
    part = (dot_right_t(d_gate, w_g) + dot_right_t(d_upper, w_u)).astype(BF16)
    pieces = [dot_left_t(normed_two, d_gate), dot_left_t(normed_two, d_upper)]
    pieces.append(dot_left_t(cot_full, hidden))
    d_normed_two, mlp_chunks = mlp_back_reduce(part, [in_chunks(p) for p in pieces])
    d_normed_two = d_normed_two.astype(F32)
    d_h1 = norm_back(d_normed_two, gains[1:2], unit_two, inverse_two) + cot_full.astype(F32)
    own_half = row * width
    d_gain_two = jnp.sum(d_normed_two * unit_two, axis=0)
    d_gain_two = lax.dynamic_slice_in_dim(d_gain_two, own_half, width)

    d_branch = d_h1.astype(BF16)
    d_heads = dot_right_t(d_branch, w_o).astype(BF16)
    d_q, d_k, d_v = [], [], []
    for query, keys, values, probs, d_out in zip(
        q_heads, k_heads, v_heads, head_probs, to_heads(d_heads)
    ):
        d_v.append(dot_left_t(probs.astype(BF16), d_out))
        d_probs = dot_right_t(d_out, values)
        d_scores = (
            probs * (d_probs - jnp.sum(probs * d_probs, axis=-1, keepdims=True))
        ).astype(BF16)
        d_q.append(rotate(dot_plain(d_scores, keys) * scale, rot_cos, -rot_sin))
        d_k.append(rotate(dot_left_t(d_scores, query) * scale, rot_cos, -rot_sin))
    d_qkv = jnp.concatenate(d_q + d_k + d_v, 1).astype(BF16)
    part = dot_right_t(d_qkv, w_qkv).astype(BF16)
    pieces = [
        in_chunks(dot_left_t(normed_one, d_qkv[:, i * own_cols : (i + 1) * own_cols]))
        for i in range(3)
    ]
    pieces.append(in_chunks(dot_left_t(d_branch, heads)))
    d_bias = jnp.sum(d_qkv.astype(F32), axis=0)
    small = jnp.zeros((8, width), F32)
    small = small.at[1].set(d_gain_two)
    small = small.at[2:5, :own_cols].set(d_bias.reshape(3, own_cols))
    unit_own = lax.dynamic_slice_in_dim(unit_one, own_half, width, 1)
    part_out = dot_plain(hidden, w_d).astype(BF16)
    d_normed_one, layer_out, small, summed = last_exchange(
        part, part_out, own_block(h1_full), unit_own, small, mlp_chunks, pieces
    )
    d_tokens = norm_back(d_normed_one.astype(F32), gains[0:1], unit_one, inverse_one) + d_h1
    d_tokens = own_block(d_tokens.astype(BF16))
    own_small = lax.dynamic_index_in_dim(small, row, 0, keepdims=False)
    bias_sum = [small[:, 2 + i, :own_cols].reshape(-1) for i in range(3)]
    summed = [from_chunks(item) for item in summed]
    return (
        layer_out,
        d_tokens,
        own_small[0],
        summed[3],
        summed[4],
        summed[5],
        bias_sum[0],
        bias_sum[1],
        bias_sum[2],
        summed[6].T,
        own_small[1],
        summed[0],
        summed[1],
        summed[2].T,
    )


def solution(mesh):
    block = P(("dp", "col"), "row")
    down, across = P("row", "col"), P("col", "row")
    return jax.shard_map(
        on_device,
        mesh=mesh,
        in_specs=(
            block,
            P("dp", None),
            P("row"),
            down,
            down,
            down,
            P("col"),
            P("col"),
            P("col"),
            across,
            P("row"),
            down,
            down,
            across,
            block,
        ),
        out_specs=(
            block,
            block,
            P("row"),
            down,
            down,
            down,
            P("col"),
            P("col"),
            P("col"),
            across,
            P("row"),
            down,
            down,
            across,
        ),
        check_vma=False,
    )
```

```python
import functools

import jax
import jax.numpy as jnp
from jax import lax
from jax.experimental import pallas as pl
from jax.experimental.pallas import tpu as pltpu
from jax.sharding import PartitionSpec as P

HEAD_DIM = 64
NORM_EPS = 1e-06
ROPE_THETA = 1000000.0
MESH = pl.DeviceIdType.MESH
F32 = jnp.float32
BF16 = jnp.bfloat16


def dot_plain(left, right):
    return jnp.dot(left, right, preferred_element_type=F32)


def dot_left_t(left, right):
    return lax.dot_general(left, right, (((0,), (0,)), ((), ())), preferred_element_type=F32)


def dot_right_t(left, right):
    return lax.dot_general(left, right, (((1,), (1,)), ((), ())), preferred_element_type=F32)


class Plane:
    def __init__(self, rows, cols):
        self.row = lax.axis_index("row")
        col = lax.axis_index("col")
        self.chip, self.core = col // 2, col % 2
        self.n_row, self.n_chip = rows, cols // 2
        self.offsets = [
            (dr, dc) for dr in range(rows) for dc in range(cols // 2) if (dr, dc) != (0, 0)
        ]

    def sibling(self):
        return {"row": self.row, "col": self.chip * 2 + 1 - self.core}

    def place(self, dr, dc, sign=1):
        return (
            lax.rem(self.row + sign * dr + self.n_row, self.n_row),
            lax.rem(self.chip + sign * dc + self.n_chip, self.n_chip),
        )

    def device(self, place):
        return {"row": place[0], "col": place[1] * 2 + self.core}

    def barrier(self, extra=()):
        sem = pltpu.get_barrier_semaphore()
        peers = [self.sibling()] + [self.device(self.place(*off)) for off in self.offsets]
        peers += list(extra)
        for peer in peers:
            pl.semaphore_signal(sem, inc=1, device_id=peer, device_id_type=MESH)
        pl.semaphore_wait(sem, len(peers))


def block_of(ref, place, core, height, width):
    top = pl.multiple_of((place[1] * 2 + core) * height, height)
    left = pl.multiple_of(place[0] * width, width)
    return ref.at[pl.ds(top, height), pl.ds(left, width)]


def remote(src, dst, send, recv, device):
    return pltpu.make_async_remote_copy(
        src_ref=src, dst_ref=dst, send_sem=send, recv_sem=recv, device_id=device, device_id_type=MESH
    )


def gather_start(plane, out, height, width, sems):
    sib_send, sib_recv, chip_send, chip_recv = sems
    here = (plane.row, plane.chip)
    own = block_of(out, here, plane.core, height, width)
    copies = []
    for k, off in enumerate(plane.offsets):
        copy = remote(own, own, chip_send.at[k], chip_recv.at[k], plane.device(plane.place(*off)))
        copy.start()
        copies.append(copy)
    last = len(plane.offsets)
    copy = remote(own, own, sib_send.at[last], sib_recv.at[last], plane.sibling())
    copy.start()
    copies.append(copy)
    return copies


def gather_end(plane, out, height, width, sems, copies):
    sib_send, sib_recv, chip_send, chip_recv = sems
    for k, off in enumerate(plane.offsets):
        block = block_of(out, plane.place(*off, sign=-1), plane.core, height, width)
        yield
        remote(block, block, chip_send.at[k], chip_recv.at[k], plane.sibling()).wait_recv()
        copy = remote(block, block, sib_send.at[k], sib_recv.at[k], plane.sibling())
        copy.start()
        copies.append(copy)
    for k, off in enumerate(plane.offsets + [(0, 0)]):
        block = block_of(out, plane.place(*off, sign=-1), 1 - plane.core, height, width)
        yield
        remote(block, block, sib_send.at[k], sib_recv.at[k], plane.sibling()).wait_recv()
    for copy in copies:
        copy.wait_send()


def run_all(*steps):
    steps = list(steps)
    while steps:
        for step in list(steps):
            try:
                next(step)
            except StopIteration:
                steps.remove(step)


def gather_kernel(rows, cols, count, *refs):
    ins, outs, sems = refs[:count], refs[count : 2 * count], refs[2 * count :]
    plane = Plane(rows, cols)
    height, width = ins[0].shape
    here = (plane.row, plane.chip)
    for src, out in zip(ins, outs):
        block_of(out, here, plane.core, height, width)[...] = src[...]
    plane.barrier()
    pending = []
    for i, out in enumerate(outs):
        own_sems = [sem.at[i] for sem in sems]
        pending.append((out, own_sems, gather_start(plane, out, height, width, own_sems)))
    run_all(*[gather_end(plane, out, height, width, own, copies) for out, own, copies in pending])


def reduce_steps(plane, part, addend, out, scratch):
    sib_buf, send_buf, recv_buf, s_send, s_recv, c_send, c_recv = scratch[:7]
    sems = scratch[7:]
    height, width = send_buf.shape[1:]
    here = (plane.row, plane.chip)
    sib_copies = []
    for dc in reversed(range(plane.n_chip)):
        chip = plane.place(0, dc)[1]
        top = pl.multiple_of((chip * 2 + 1 - plane.core) * height, height)
        copy = remote(
            part.at[pl.ds(top, height), :],
            sib_buf.at[dc],
            s_send.at[dc],
            s_recv.at[dc],
            plane.sibling(),
        )
        copy.start()
        sib_copies.append(copy)

    def both(place, dc):
        left = pl.multiple_of(place[0] * width, width)
        own = block_of(part, place, plane.core, height, width)[...]
        return own.astype(F32) + sib_buf[dc, :, pl.ds(left, width)].astype(F32)

    copies = []
    waited = set()
    order = sorted(range(len(plane.offsets)), key=lambda k: (-plane.offsets[k][1], -plane.offsets[k][0]))
    for k in order:
        dr, dc = plane.offsets[k]
        if dc not in waited:
            waited.add(dc)
            yield
            sib_copies[plane.n_chip - 1 - dc].wait_recv()
        place = plane.place(dr, dc)
        send_buf[k] = both(place, dc).astype(BF16)
        copy = remote(
            send_buf.at[k], recv_buf.at[k], c_send.at[k], c_recv.at[k], plane.device(place)
        )
        copy.start()
        copies.append(copy)
    if 0 not in waited:
        sib_copies[plane.n_chip - 1].wait_recv()
    total = both(here, 0)
    if addend is not None:
        total = total + addend[...].astype(F32)
    for copy in copies:
        yield
        copy.wait_recv()
    for k in range(len(plane.offsets)):
        total = total + recv_buf[k].astype(F32)
    if sems:
        block_of(out, here, plane.core, height, width)[...] = total.astype(out.dtype)
        pending = gather_start(plane, out, height, width, sems)
        yield from gather_end(plane, out, height, width, sems, pending)
    else:
        out[...] = total.astype(out.dtype)
    for copy in copies + sib_copies:
        copy.wait_send()


def reduce_kernel(rows, cols, part, addend, out, *scratch):
    plane = Plane(rows, cols)
    plane.barrier()
    run_all(reduce_steps(plane, part, addend, out, scratch))


class Ring:
    def __init__(self, count, sign=1):
        self.count, self.sign = count, sign
        self.place = lax.axis_index("dp")
        self.next = {"dp": self.at(1)}

    def at(self, offset):
        return lax.rem(self.place + self.sign * offset + 2 * self.count, self.count)


def ring_sum_steps(ring, pieces, out, recv, send_sem, recv_sem):
    copies = []
    for step in range(ring.count - 1):
        if step == 0:
            src = pieces.at[:, ring.at(-1)]
        else:
            src = recv.at[step - 1]
        copy = remote(src, recv.at[step], send_sem.at[step], recv_sem.at[step], ring.next)
        copy.start()
        copies.append(copy)
        yield
        copy.wait_recv()
        total = recv[step].astype(F32) + pieces[:, ring.at(-step - 2)].astype(F32)
        if step < ring.count - 2:
            recv[step] = total.astype(BF16)
        else:
            out[...] = total.astype(BF16)
    for copy in copies:
        copy.wait_send()


def ring_gather_steps(ring, plane, chunk, out, row_sems, send_sem, recv_sem):
    swap = remote(
        chunk.at[1 - plane.row],
        out.at[ring.place, plane.row],
        row_sems.at[0],
        row_sems.at[1],
        plane.device((1 - plane.row, plane.chip)),
    )
    swap.start()
    out[ring.place, plane.row] = chunk[plane.row]
    yield
    landed = out.at[ring.place, 1 - plane.row]
    remote(landed, landed, row_sems.at[0], row_sems.at[1], ring.next).wait_recv()
    copies = [swap]
    for step in range(ring.count - 1):
        src = out.at[ring.at(-step)]
        copy = remote(src, src, send_sem.at[step], recv_sem.at[step], ring.next)
        copy.start()
        copies.append(copy)
        yield
        came = out.at[ring.at(-step - 1)]
        remote(came, came, send_sem.at[step], recv_sem.at[step], ring.next).wait_recv()
    for copy in copies:
        copy.wait_send()


def mlp_kernel(rows, cols, count, pieces_count, *refs):
    part, pieces = refs[0], refs[1 : 1 + pieces_count]
    refs = refs[1 + pieces_count :]
    out, chunks = refs[0], refs[1 : 1 + pieces_count]
    refs = refs[1 + pieces_count :]
    recvs, refs = refs[:pieces_count], refs[pieces_count:]
    ring_send, ring_recv = refs[:2]
    plane, ring = Plane(rows, cols), Ring(count)
    rings = [ring, Ring(count, -1)]
    plane.barrier([ring.next, {"dp": ring.at(-1)}])
    run_all(
        reduce_steps(plane, part, None, out, refs[2:]),
        *[
            ring_sum_steps(rings[i % 2], piece, chunk, recv, ring_send.at[i], ring_recv.at[i])
            for i, (piece, chunk, recv) in enumerate(zip(pieces, chunks, recvs))
        ],
    )


def last_kernel(rows, cols, count, n_mlp, n_att, *refs):
    refs = list(refs)

    def take(number):
        taken = refs[:number]
        del refs[:number]
        return taken

    part, part_out, h1_block, unit, small = take(5)
    mlp_chunks, pieces = take(n_mlp), take(n_att)
    d_normed, layer_out, small_out = take(3)
    mlp_outs, att_outs = take(n_mlp), take(n_att)
    recvs, chunks = take(n_att), take(n_att)
    small_buf, small_send, small_recv, small_row = take(4)
    row_sems, gather_send, gather_recv, ring_send, ring_recv = take(5)
    normed_scratch, out_scratch = take(11), take(7)
    plane, ring = Plane(rows, cols), Ring(count)
    rings = [ring, Ring(count, -1)]
    others = [{"dp": ring.at(i)} for i in range(1, count)]
    plane.barrier(others)
    width = h1_block.shape[1]

    def attention(i):
        yield from ring_sum_steps(
            rings[(n_mlp + i) % 2], pieces[i], chunks[i], recvs[i], ring_send.at[i], ring_recv.at[i]
        )
        k = n_mlp + i
        yield from ring_gather_steps(
            rings[(n_mlp + i) % 2], plane, chunks[i], att_outs[i], row_sems.at[k], gather_send.at[k], gather_recv.at[k]
        )

    def normed():
        yield from reduce_steps(plane, part, None, d_normed, normed_scratch)
        left = pl.multiple_of(plane.row * width, width)
        gain = jnp.sum(d_normed[:, pl.ds(left, width)].astype(F32) * unit[...], axis=0, keepdims=True)
        first = lax.broadcasted_iota(jnp.int32, small.shape, 0) == 0
        small_buf[0] = jnp.where(first, gain, small[...])
        copies = []
        for i, other in enumerate(others):
            copy = remote(
                small_buf.at[0], small_buf.at[i + 1], small_send.at[i], small_recv.at[i], other
            )
            copy.start()
            copies.append(copy)
        for copy in copies:
            yield
            copy.wait()
        total = small_buf[0]
        for i in range(1, count):
            total = total + small_buf[i]
        small_out[plane.row] = total
        here = small_out.at[plane.row]
        pair = plane.device((1 - plane.row, plane.chip))
        copy = remote(here, here, small_row.at[0], small_row.at[1], pair)
        copy.start()
        yield
        there = small_out.at[1 - plane.row]
        remote(there, there, small_row.at[0], small_row.at[1], pair).wait_recv()
        copy.wait_send()

    gathers = [
        ring_gather_steps(
            rings[i % 2], plane, mlp_chunks[i], mlp_outs[i], row_sems.at[i], gather_send.at[i], gather_recv.at[i]
        )
        for i in range(n_mlp)
    ]
    run_all(
        *[attention(i) for i in range(n_att)],
        *gathers,
        normed(),
        reduce_steps(plane, part_out, h1_block, layer_out, out_scratch),
    )


def dma(*shape):
    return pltpu.SemaphoreType.DMA(shape)


def params(collective_id):
    return pltpu.CompilerParams(
        collective_id=collective_id, has_side_effects=True, vmem_limit_bytes=32 << 20
    )


VMEM = pl.BlockSpec(memory_space=pltpu.VMEM)


def plane_gather(blocks, collective_id):
    rows, cols = lax.axis_size("row"), lax.axis_size("col")
    chips = rows * cols // 2
    count = len(blocks)
    height, width = blocks[0].shape
    return pl.pallas_call(
        functools.partial(gather_kernel, rows, cols, count),
        out_shape=[jax.ShapeDtypeStruct((height * cols, width * rows), b.dtype) for b in blocks],
        in_specs=[VMEM] * count,
        out_specs=[VMEM] * count,
        scratch_shapes=[dma(count, chips), dma(count, chips), dma(count, chips), dma(count, chips)],
        compiler_params=params(collective_id),
        name=f"plane_gather_{collective_id}",
    )(*blocks)


def reduce_scratch(rows, cols, height, width, gather):
    chips = rows * cols // 2
    scratch = [
        pltpu.VMEM((cols // 2, height, width * rows), BF16),
        pltpu.VMEM((chips - 1, height, width), BF16),
        pltpu.VMEM((chips - 1, height, width), BF16),
        dma(cols // 2),
        dma(cols // 2),
        dma(chips - 1),
        dma(chips - 1),
    ]
    if gather:
        scratch += [dma(chips), dma(chips), dma(chips), dma(chips)]
    return scratch


def call(kernel, ins, outs, scratch, collective_id, name):
    return pl.pallas_call(
        kernel,
        out_shape=outs,
        in_specs=[VMEM] * len(ins),
        out_specs=[VMEM] * len(outs),
        scratch_shapes=scratch,
        compiler_params=params(collective_id),
        name=name,
    )(*ins)


def shape(dims, dtype=BF16):
    return jax.ShapeDtypeStruct(tuple(dims), dtype)


def plane_reduce(part, addend):
    rows, cols = lax.axis_size("row"), lax.axis_size("col")
    height, width = addend.shape
    return call(
        functools.partial(reduce_kernel, rows, cols),
        [part, addend],
        [shape(part.shape)],
        reduce_scratch(rows, cols, height, width, True),
        1,
        "out_projection_reduce",
    )[0]


def mlp_back_reduce(part, pieces):
    rows, cols, count = lax.axis_size("row"), lax.axis_size("col"), lax.axis_size("dp")
    height, width = part.shape[0] // cols, part.shape[1] // rows
    chunks = [(p.shape[0],) + p.shape[2:] for p in pieces]
    scratch = [pltpu.VMEM((count - 1,) + c, BF16) for c in chunks]
    scratch += [dma(len(pieces), count - 1), dma(len(pieces), count - 1)]
    scratch += reduce_scratch(rows, cols, height, width, True)
    outs = call(
        functools.partial(mlp_kernel, rows, cols, count, len(pieces)),
        [part] + pieces,
        [shape(part.shape)] + [shape(c) for c in chunks],
        scratch,
        2,
        "mlp_back_reduce",
    )
    return outs[0], list(outs[1:])


def last_exchange(part, part_out, h1_block, unit, small, mlp_chunks, pieces):
    rows, cols, count = lax.axis_size("row"), lax.axis_size("col"), lax.axis_size("dp")
    height, width = h1_block.shape
    n_mlp, n_att = len(mlp_chunks), len(pieces)
    chunks = [(p.shape[0],) + p.shape[2:] for p in pieces]
    outs = [shape(part.shape), shape(h1_block.shape), shape((rows,) + small.shape, F32)]
    outs += [shape((count,) + c.shape) for c in mlp_chunks]
    outs += [shape((count,) + c) for c in chunks]
    scratch = [pltpu.VMEM((count - 1,) + c, BF16) for c in chunks]
    scratch += [pltpu.VMEM(c, BF16) for c in chunks]
    scratch += [pltpu.VMEM((count,) + small.shape, F32), dma(count - 1), dma(count - 1), dma(2)]
    scratch += [dma(n_mlp + n_att, 2), dma(n_mlp + n_att, count - 1), dma(n_mlp + n_att, count - 1)]
    scratch += [dma(n_att, count - 1), dma(n_att, count - 1)]
    scratch += reduce_scratch(rows, cols, height, width, True)
    scratch += reduce_scratch(rows, cols, height, width, False)
    outs = call(
        functools.partial(last_kernel, rows, cols, count, n_mlp, n_att),
        [part, part_out, h1_block, unit, small] + mlp_chunks + pieces,
        outs,
        scratch,
        3,
        "last_exchange",
    )
    return outs[0], outs[1], outs[2], outs[3:]


def swap_rows(value):
    return lax.ppermute(value, "row", [(0, 1), (1, 0)])


def half_of(value, index, axis):
    size = value.shape[axis] // 2
    return lax.dynamic_slice_in_dim(value, index * size, size, axis)


def in_order(row, own, other, axis):
    return jnp.where(
        row == 0,
        jnp.concatenate([own, other], axis),
        jnp.concatenate([other, own], axis),
    )


def whole_of_half(weight, row, cut, join):
    other = swap_rows(half_of(weight, 1 - row, cut))
    return in_order(row, half_of(weight, row, cut), other, join)


def unit_of(values):
    inverse = lax.rsqrt(jnp.mean(values * values, axis=1, keepdims=True) + NORM_EPS)
    return values * inverse, inverse


def norm_back(d_normed, gain, unit, inverse):
    scaled = d_normed * gain
    inner = jnp.sum(scaled * unit, axis=1, keepdims=True)
    return inverse * (scaled - unit * (inner / unit.shape[1]))


def layout(lengths, group_len):
    seq_ends = jnp.cumsum(lengths)
    token_place = jnp.arange(group_len, dtype=jnp.int32)
    seq_ids = jnp.sum((token_place[:, None] >= seq_ends[None, :]).astype(jnp.int32), axis=1)
    seq_starts = seq_ends - lengths
    onehot = (seq_ids[:, None] == jnp.arange(lengths.shape[0], dtype=jnp.int32)[None, :]).astype(
        jnp.int32
    )
    position = token_place - jnp.sum(onehot * seq_starts[None, :], axis=1)
    allowed = (seq_ids[:, None] == seq_ids[None, :]) & (
        token_place[None, :] <= token_place[:, None]
    )
    freqs = ROPE_THETA ** (-(jnp.arange(HEAD_DIM // 2, dtype=F32) * 2.0 / HEAD_DIM))
    angles = position.astype(F32)[:, None] * freqs[None, :]
    return (jnp.cos(angles), jnp.sin(angles), allowed)


def rotate(values, rot_cos, rot_sin):
    half_dim = HEAD_DIM // 2
    first, second = values[..., :half_dim], values[..., half_dim:]
    return jnp.concatenate(
        [first * rot_cos - second * rot_sin, second * rot_cos + first * rot_sin], axis=-1
    )


def to_heads(values):
    return [values[:, i : i + HEAD_DIM] for i in range(0, values.shape[1], HEAD_DIM)]


def in_chunks(grad):
    count = lax.axis_size("dp")
    grad = grad.astype(BF16)
    return grad.reshape(2, count, grad.shape[0] // (2 * count), grad.shape[1])


def from_chunks(summed, turned):
    halves = [summed[:, i].reshape(-1, summed.shape[3]).astype(F32) for i in range(2)]
    return jnp.concatenate([half.T for half in halves]) if turned else jnp.concatenate(halves, 1)


def on_device(
    tokens,
    seq_lengths,
    norm1_gain,
    w_query,
    w_key,
    w_value,
    b_query,
    b_key,
    b_value,
    w_out,
    norm2_gain,
    w_gate,
    w_up,
    w_down,
    cotangent,
):
    height, width = tokens.shape
    row, col = lax.axis_index("row"), lax.axis_index("col")
    rows, cols = lax.axis_size("row"), lax.axis_size("col")
    group_len = height * cols
    scale = HEAD_DIM ** (-0.5)

    def own_block(full):
        return lax.dynamic_slice(full, (col * height, row * width), (height, width))

    def joined_half(parts):
        return jnp.concatenate([half_of(part, row, 0) for part in parts])

    w_qkv_own = jnp.concatenate([half_of(w, row, 1) for w in (w_query, w_key, w_value)], 1)
    w_qkv_other = swap_rows(
        jnp.concatenate([half_of(w, 1 - row, 1) for w in (w_query, w_key, w_value)], 1)
    )
    w_qkv = in_order(row, w_qkv_own, w_qkv_other, 0)
    gains = jnp.stack([norm1_gain, norm2_gain])
    gains = in_order(row, gains, swap_rows(gains), 1)
    w_o = whole_of_half(w_out, row, 0, 1)

    token_full, cot_full = plane_gather([tokens, cotangent], 0)
    token_full, w_gate, w_up, w_down = lax.optimization_barrier((token_full, w_gate, w_up, w_down))
    w_g = whole_of_half(w_gate, row, 1, 0)
    w_u = whole_of_half(w_up, row, 1, 0)
    w_d = whole_of_half(w_down, row, 0, 1)
    resid = token_full.astype(F32)
    unit_one, inverse_one = unit_of(resid)
    normed_one = (unit_one * gains[0:1]).astype(BF16)
    qkv = dot_plain(normed_one, w_qkv) + joined_half((b_query, b_key, b_value))
    own_cols = qkv.shape[1] // 3
    rot_cos, rot_sin, allowed = layout(seq_lengths[0], group_len)
    q_heads = [rotate(h, rot_cos, rot_sin).astype(BF16) for h in to_heads(qkv[:, :own_cols])]
    k_heads = [
        rotate(h, rot_cos, rot_sin).astype(BF16) for h in to_heads(qkv[:, own_cols : 2 * own_cols])
    ]
    v_heads = [h.astype(BF16) for h in to_heads(qkv[:, 2 * own_cols :])]
    head_outs, head_probs = [], []
    for query, keys, values in zip(q_heads, k_heads, v_heads):
        scores = jnp.where(allowed, dot_right_t(query, keys) * scale, -1000000000.0)
        expo = jnp.exp(scores - jnp.max(scores, axis=-1, keepdims=True))
        probs = expo / jnp.sum(expo, axis=-1, keepdims=True)
        head_probs.append(probs)
        head_outs.append(dot_plain(probs.astype(BF16), values).astype(BF16))
    heads = jnp.concatenate(head_outs, 1)
    h1_full = plane_reduce(dot_plain(heads, w_o).astype(BF16), tokens)
    unit_two, inverse_two = unit_of(h1_full.astype(F32))
    normed_two = (unit_two * gains[1:2]).astype(BF16)
    gate, upper = dot_plain(normed_two, w_g), dot_plain(normed_two, w_u)
    sigmoid_gate = jax.nn.sigmoid(gate)
    silu_gate = gate * sigmoid_gate
    hidden = (silu_gate * upper).astype(BF16)
    d_hidden = dot_right_t(cot_full, w_d).astype(BF16).astype(F32)
    d_gate = (d_hidden * upper * sigmoid_gate * (1.0 + gate * (1.0 - sigmoid_gate))).astype(BF16)
    d_upper = (d_hidden * silu_gate).astype(BF16)
    part = (dot_right_t(d_gate, w_g) + dot_right_t(d_upper, w_u)).astype(BF16)
    pieces = [dot_left_t(normed_two, d_gate), dot_left_t(normed_two, d_upper)]
    pieces.append(dot_left_t(cot_full, hidden))
    d_normed_two, mlp_chunks = mlp_back_reduce(part, [in_chunks(p) for p in pieces])
    d_normed_two = d_normed_two.astype(F32)
    d_h1 = norm_back(d_normed_two, gains[1:2], unit_two, inverse_two) + cot_full.astype(F32)
    own_half = row * width
    d_gain_two = jnp.sum(d_normed_two * unit_two, axis=0)
    d_gain_two = lax.dynamic_slice_in_dim(d_gain_two, own_half, width)

    d_branch = d_h1.astype(BF16)
    d_heads = dot_right_t(d_branch, w_o).astype(BF16)
    d_q, d_k, d_v = [], [], []
    for query, keys, values, probs, d_out in zip(
        q_heads, k_heads, v_heads, head_probs, to_heads(d_heads)
    ):
        d_v.append(dot_left_t(probs.astype(BF16), d_out))
        d_probs = dot_right_t(d_out, values)
        d_scores = (
            probs * (d_probs - jnp.sum(probs * d_probs, axis=-1, keepdims=True))
        ).astype(BF16)
        d_q.append(rotate(dot_plain(d_scores, keys) * scale, rot_cos, -rot_sin))
        d_k.append(rotate(dot_left_t(d_scores, query) * scale, rot_cos, -rot_sin))
    d_qkv = jnp.concatenate(d_q + d_k + d_v, 1).astype(BF16)
    part = dot_right_t(d_qkv, w_qkv).astype(BF16)
    pieces = [
        in_chunks(dot_left_t(normed_one, d_qkv[:, i * own_cols : (i + 1) * own_cols]))
        for i in range(3)
    ]
    pieces.append(in_chunks(dot_left_t(d_branch, heads)))
    d_bias = jnp.sum(d_qkv.astype(F32), axis=0)
    small = jnp.zeros((8, width), F32)
    small = small.at[1].set(d_gain_two)
    small = small.at[2:5, :own_cols].set(d_bias.reshape(3, own_cols))
    unit_own = lax.dynamic_slice_in_dim(unit_one, own_half, width, 1)
    part_out = dot_plain(hidden, w_d).astype(BF16)
    d_normed_one, layer_out, small, summed = last_exchange(
        part, part_out, own_block(h1_full), unit_own, small, mlp_chunks, pieces
    )
    d_tokens = norm_back(d_normed_one.astype(F32), gains[0:1], unit_one, inverse_one) + d_h1
    d_tokens = own_block(d_tokens.astype(BF16))
    own_small = lax.dynamic_index_in_dim(small, row, 0, keepdims=False)
    bias_sum = [small[:, 2 + i, :own_cols].reshape(-1) for i in range(3)]
    summed = [from_chunks(item, i in (2, 6)) for i, item in enumerate(summed)]
    return (
        layer_out,
        d_tokens,
        own_small[0],
        summed[3],
        summed[4],
        summed[5],
        bias_sum[0],
        bias_sum[1],
        bias_sum[2],
        summed[6],
        own_small[1],
        summed[0],
        summed[1],
        summed[2],
    )


def solution(mesh):
    block = P(("dp", "col"), "row")
    down, across = P("row", "col"), P("col", "row")
    return jax.shard_map(
        on_device,
        mesh=mesh,
        in_specs=(
            block,
            P("dp", None),
            P("row"),
            down,
            down,
            down,
            P("col"),
            P("col"),
            P("col"),
            across,
            P("row"),
            down,
            down,
            across,
            block,
        ),
        out_specs=(
            block,
            block,
            P("row"),
            down,
            down,
            down,
            P("col"),
            P("col"),
            P("col"),
            across,
            P("row"),
            down,
            down,
            across,
        ),
        check_vma=False,
    )
```

```python
import functools

import jax
import jax.numpy as jnp
from jax import lax
from jax.experimental import pallas as pl
from jax.experimental.pallas import tpu as pltpu
from jax.sharding import PartitionSpec as P

HEAD_DIM = 64
NORM_EPS = 1e-06
ROPE_THETA = 1000000.0
MESH = pl.DeviceIdType.MESH
F32 = jnp.float32
BF16 = jnp.bfloat16


def dot_plain(left, right):
    return jnp.dot(left, right, preferred_element_type=F32)


def dot_left_t(left, right):
    return lax.dot_general(left, right, (((0,), (0,)), ((), ())), preferred_element_type=F32)


def dot_right_t(left, right):
    return lax.dot_general(left, right, (((1,), (1,)), ((), ())), preferred_element_type=F32)


class Plane:
    def __init__(self, rows, cols):
        self.row = lax.axis_index("row")
        col = lax.axis_index("col")
        self.chip, self.core = col // 2, col % 2
        self.n_row, self.n_chip = rows, cols // 2
        self.offsets = [
            (dr, dc) for dr in range(rows) for dc in range(cols // 2) if (dr, dc) != (0, 0)
        ]

    def sibling(self):
        return {"row": self.row, "col": self.chip * 2 + 1 - self.core}

    def place(self, dr, dc, sign=1):
        return (
            lax.rem(self.row + sign * dr + self.n_row, self.n_row),
            lax.rem(self.chip + sign * dc + self.n_chip, self.n_chip),
        )

    def device(self, place):
        return {"row": place[0], "col": place[1] * 2 + self.core}

    def barrier(self, extra=()):
        sem = pltpu.get_barrier_semaphore()
        peers = [self.sibling()] + [self.device(self.place(*off)) for off in self.offsets]
        peers += list(extra)
        for peer in peers:
            pl.semaphore_signal(sem, inc=1, device_id=peer, device_id_type=MESH)
        pl.semaphore_wait(sem, len(peers))


def block_of(ref, place, core, height, width):
    top = pl.multiple_of((place[1] * 2 + core) * height, height)
    left = pl.multiple_of(place[0] * width, width)
    return ref.at[pl.ds(top, height), pl.ds(left, width)]


def remote(src, dst, send, recv, device):
    return pltpu.make_async_remote_copy(
        src_ref=src, dst_ref=dst, send_sem=send, recv_sem=recv, device_id=device, device_id_type=MESH
    )


def gather_start(plane, out, height, width, sems):
    sib_send, sib_recv, chip_send, chip_recv = sems
    here = (plane.row, plane.chip)
    own = block_of(out, here, plane.core, height, width)
    copies = []
    for k, off in enumerate(plane.offsets):
        copy = remote(own, own, chip_send.at[k], chip_recv.at[k], plane.device(plane.place(*off)))
        copy.start()
        copies.append(copy)
    last = len(plane.offsets)
    copy = remote(own, own, sib_send.at[last], sib_recv.at[last], plane.sibling())
    copy.start()
    copies.append(copy)
    return copies


def gather_end(plane, out, height, width, sems, copies):
    sib_send, sib_recv, chip_send, chip_recv = sems
    for k, off in enumerate(plane.offsets):
        block = block_of(out, plane.place(*off, sign=-1), plane.core, height, width)
        yield
        remote(block, block, chip_send.at[k], chip_recv.at[k], plane.sibling()).wait_recv()
        copy = remote(block, block, sib_send.at[k], sib_recv.at[k], plane.sibling())
        copy.start()
        copies.append(copy)
    for k, off in enumerate(plane.offsets + [(0, 0)]):
        block = block_of(out, plane.place(*off, sign=-1), 1 - plane.core, height, width)
        yield
        remote(block, block, sib_send.at[k], sib_recv.at[k], plane.sibling()).wait_recv()
    for copy in copies:
        copy.wait_send()


def run_all(*steps):
    steps = list(steps)
    while steps:
        for step in list(steps):
            try:
                next(step)
            except StopIteration:
                steps.remove(step)


def gather_kernel(rows, cols, count, *refs):
    ins, outs, sems = refs[:count], refs[count : 2 * count], refs[2 * count :]
    plane = Plane(rows, cols)
    height, width = ins[0].shape
    here = (plane.row, plane.chip)
    for src, out in zip(ins, outs):
        block_of(out, here, plane.core, height, width)[...] = src[...]
    plane.barrier()
    pending = []
    for i, out in enumerate(outs):
        own_sems = [sem.at[i] for sem in sems]
        pending.append((out, own_sems, gather_start(plane, out, height, width, own_sems)))
    run_all(*[gather_end(plane, out, height, width, own, copies) for out, own, copies in pending])


def reduce_steps(plane, part, addend, out, scratch):
    sib_buf, send_buf, recv_buf, s_send, s_recv, c_send, c_recv = scratch[:7]
    sems = scratch[7:]
    height, width = send_buf.shape[1:]
    here = (plane.row, plane.chip)
    sib_copies = []
    for dc in reversed(range(plane.n_chip)):
        chip = plane.place(0, dc)[1]
        top = pl.multiple_of((chip * 2 + 1 - plane.core) * height, height)
        copy = remote(
            part.at[pl.ds(top, height), :],
            sib_buf.at[dc],
            s_send.at[dc],
            s_recv.at[dc],
            plane.sibling(),
        )
        copy.start()
        sib_copies.append(copy)

    def both(place, dc):
        left = pl.multiple_of(place[0] * width, width)
        own = block_of(part, place, plane.core, height, width)[...]
        return own.astype(F32) + sib_buf[dc, :, pl.ds(left, width)].astype(F32)

    copies = []
    waited = set()
    order = sorted(range(len(plane.offsets)), key=lambda k: (-plane.offsets[k][1], -plane.offsets[k][0]))
    for k in order:
        dr, dc = plane.offsets[k]
        if dc not in waited:
            waited.add(dc)
            yield
            sib_copies[plane.n_chip - 1 - dc].wait_recv()
        place = plane.place(dr, dc)
        send_buf[k] = both(place, dc).astype(BF16)
        copy = remote(
            send_buf.at[k], recv_buf.at[k], c_send.at[k], c_recv.at[k], plane.device(place)
        )
        copy.start()
        copies.append(copy)
    if 0 not in waited:
        sib_copies[plane.n_chip - 1].wait_recv()
    total = both(here, 0)
    if addend is not None:
        total = total + addend[...].astype(F32)
    for copy in copies:
        yield
        copy.wait_recv()
    for k in range(len(plane.offsets)):
        total = total + recv_buf[k].astype(F32)
    if sems:
        block_of(out, here, plane.core, height, width)[...] = total.astype(out.dtype)
        pending = gather_start(plane, out, height, width, sems)
        yield from gather_end(plane, out, height, width, sems, pending)
    else:
        out[...] = total.astype(out.dtype)
    for copy in copies + sib_copies:
        copy.wait_send()


def reduce_kernel(rows, cols, part, addend, out, *scratch):
    plane = Plane(rows, cols)
    plane.barrier()
    run_all(reduce_steps(plane, part, addend, out, scratch))


class Ring:
    def __init__(self, count, sign=1):
        self.count, self.sign = count, sign
        self.place = lax.axis_index("dp")
        self.next = {"dp": self.at(1)}

    def at(self, offset):
        return lax.rem(self.place + self.sign * offset + 2 * self.count, self.count)


def ring_sum_steps(ring, pieces, out, recv, send_sem, recv_sem):
    copies = []
    for step in range(ring.count - 1):
        if step == 0:
            src = pieces.at[:, ring.at(-1)]
        else:
            src = recv.at[step - 1]
        copy = remote(src, recv.at[step], send_sem.at[step], recv_sem.at[step], ring.next)
        copy.start()
        copies.append(copy)
        yield
        copy.wait_recv()
        total = recv[step].astype(F32) + pieces[:, ring.at(-step - 2)].astype(F32)
        if step < ring.count - 2:
            recv[step] = total.astype(BF16)
        else:
            out[...] = total.astype(BF16)
    for copy in copies:
        copy.wait_send()


def ring_gather_steps(ring, plane, chunk, out, row_sems, send_sem, recv_sem):
    swap = remote(
        chunk.at[1 - plane.row],
        out.at[ring.place, plane.row],
        row_sems.at[0],
        row_sems.at[1],
        plane.device((1 - plane.row, plane.chip)),
    )
    swap.start()
    out[ring.place, plane.row] = chunk[plane.row]
    yield
    landed = out.at[ring.place, 1 - plane.row]
    remote(landed, landed, row_sems.at[0], row_sems.at[1], ring.next).wait_recv()
    copies = [swap]
    for step in range(ring.count - 1):
        src = out.at[ring.at(-step)]
        copy = remote(src, src, send_sem.at[step], recv_sem.at[step], ring.next)
        copy.start()
        copies.append(copy)
        yield
        came = out.at[ring.at(-step - 1)]
        remote(came, came, send_sem.at[step], recv_sem.at[step], ring.next).wait_recv()
    for copy in copies:
        copy.wait_send()


def mlp_kernel(rows, cols, count, pieces_count, *refs):
    part, pieces = refs[0], refs[1 : 1 + pieces_count]
    refs = refs[1 + pieces_count :]
    out, chunks = refs[0], refs[1 : 1 + pieces_count]
    refs = refs[1 + pieces_count :]
    recvs, refs = refs[:pieces_count], refs[pieces_count:]
    ring_send, ring_recv = refs[:2]
    plane, ring = Plane(rows, cols), Ring(count)
    rings = [ring, Ring(count, -1)]
    plane.barrier([ring.next, {"dp": ring.at(-1)}])
    run_all(
        reduce_steps(plane, part, None, out, refs[2:]),
        *[
            ring_sum_steps(rings[i % 2], piece, chunk, recv, ring_send.at[i], ring_recv.at[i])
            for i, (piece, chunk, recv) in enumerate(zip(pieces, chunks, recvs))
        ],
    )


def last_kernel(rows, cols, count, n_mlp, n_att, *refs):
    refs = list(refs)

    def take(number):
        taken = refs[:number]
        del refs[:number]
        return taken

    part, part_out, h1_block, unit, small = take(5)
    mlp_chunks, pieces = take(n_mlp), take(n_att)
    d_normed, layer_out, small_out = take(3)
    mlp_outs, att_outs = take(n_mlp), take(n_att)
    recvs, chunks = take(n_att), take(n_att)
    small_buf, small_send, small_recv, small_row = take(4)
    row_sems, gather_send, gather_recv, ring_send, ring_recv = take(5)
    normed_scratch, out_scratch = take(11), take(7)
    plane, ring = Plane(rows, cols), Ring(count)
    rings = [ring, Ring(count, -1)]
    others = [{"dp": ring.at(i)} for i in range(1, count)]
    plane.barrier(others)
    width = h1_block.shape[1]

    def attention(i):
        yield from ring_sum_steps(
            rings[(n_mlp + i) % 2], pieces[i], chunks[i], recvs[i], ring_send.at[i], ring_recv.at[i]
        )
        k = n_mlp + i
        yield from ring_gather_steps(
            rings[(n_mlp + i) % 2], plane, chunks[i], att_outs[i], row_sems.at[k], gather_send.at[k], gather_recv.at[k]
        )

    def normed():
        yield from reduce_steps(plane, part, None, d_normed, normed_scratch)
        left = pl.multiple_of(plane.row * width, width)
        gain = jnp.sum(d_normed[:, pl.ds(left, width)].astype(F32) * unit[...], axis=0, keepdims=True)
        first = lax.broadcasted_iota(jnp.int32, small.shape, 0) == 0
        small_buf[0] = jnp.where(first, gain, small[...])
        copies = []
        for i, other in enumerate(others):
            copy = remote(
                small_buf.at[0], small_buf.at[i + 1], small_send.at[i], small_recv.at[i], other
            )
            copy.start()
            copies.append(copy)
        for copy in copies:
            yield
            copy.wait()
        total = small_buf[0]
        for i in range(1, count):
            total = total + small_buf[i]
        small_out[plane.row] = total
        here = small_out.at[plane.row]
        pair = plane.device((1 - plane.row, plane.chip))
        copy = remote(here, here, small_row.at[0], small_row.at[1], pair)
        copy.start()
        yield
        there = small_out.at[1 - plane.row]
        remote(there, there, small_row.at[0], small_row.at[1], pair).wait_recv()
        copy.wait_send()

    gathers = [
        ring_gather_steps(
            rings[i % 2], plane, mlp_chunks[i], mlp_outs[i], row_sems.at[i], gather_send.at[i], gather_recv.at[i]
        )
        for i in range(n_mlp)
    ]
    run_all(
        *[attention(i) for i in range(n_att)],
        *gathers,
        normed(),
        reduce_steps(plane, part_out, h1_block, layer_out, out_scratch),
    )


def dma(*shape):
    return pltpu.SemaphoreType.DMA(shape)


def params(collective_id):
    return pltpu.CompilerParams(
        collective_id=collective_id, has_side_effects=True, vmem_limit_bytes=32 << 20
    )


VMEM = pl.BlockSpec(memory_space=pltpu.VMEM)


def plane_gather(blocks, collective_id):
    rows, cols = lax.axis_size("row"), lax.axis_size("col")
    chips = rows * cols // 2
    count = len(blocks)
    height, width = blocks[0].shape
    return pl.pallas_call(
        functools.partial(gather_kernel, rows, cols, count),
        out_shape=[jax.ShapeDtypeStruct((height * cols, width * rows), b.dtype) for b in blocks],
        in_specs=[VMEM] * count,
        out_specs=[VMEM] * count,
        scratch_shapes=[dma(count, chips), dma(count, chips), dma(count, chips), dma(count, chips)],
        compiler_params=params(collective_id),
        name=f"plane_gather_{collective_id}",
    )(*blocks)


def reduce_scratch(rows, cols, height, width, gather):
    chips = rows * cols // 2
    scratch = [
        pltpu.VMEM((cols // 2, height, width * rows), BF16),
        pltpu.VMEM((chips - 1, height, width), BF16),
        pltpu.VMEM((chips - 1, height, width), BF16),
        dma(cols // 2),
        dma(cols // 2),
        dma(chips - 1),
        dma(chips - 1),
    ]
    if gather:
        scratch += [dma(chips), dma(chips), dma(chips), dma(chips)]
    return scratch


def call(kernel, ins, outs, scratch, collective_id, name):
    return pl.pallas_call(
        kernel,
        out_shape=outs,
        in_specs=[VMEM] * len(ins),
        out_specs=[VMEM] * len(outs),
        scratch_shapes=scratch,
        compiler_params=params(collective_id),
        name=name,
    )(*ins)


def shape(dims, dtype=BF16):
    return jax.ShapeDtypeStruct(tuple(dims), dtype)


def plane_reduce(part, addend):
    rows, cols = lax.axis_size("row"), lax.axis_size("col")
    height, width = addend.shape
    return call(
        functools.partial(reduce_kernel, rows, cols),
        [part, addend],
        [shape(part.shape)],
        reduce_scratch(rows, cols, height, width, True),
        1,
        "out_projection_reduce",
    )[0]


def mlp_back_reduce(part, pieces):
    rows, cols, count = lax.axis_size("row"), lax.axis_size("col"), lax.axis_size("dp")
    height, width = part.shape[0] // cols, part.shape[1] // rows
    chunks = [(p.shape[0],) + p.shape[2:] for p in pieces]
    scratch = [pltpu.VMEM((count - 1,) + c, BF16) for c in chunks]
    scratch += [dma(len(pieces), count - 1), dma(len(pieces), count - 1)]
    scratch += reduce_scratch(rows, cols, height, width, True)
    outs = call(
        functools.partial(mlp_kernel, rows, cols, count, len(pieces)),
        [part] + pieces,
        [shape(part.shape)] + [shape(c) for c in chunks],
        scratch,
        2,
        "mlp_back_reduce",
    )
    return outs[0], list(outs[1:])


def last_exchange(part, part_out, h1_block, unit, small, mlp_chunks, pieces):
    rows, cols, count = lax.axis_size("row"), lax.axis_size("col"), lax.axis_size("dp")
    height, width = h1_block.shape
    n_mlp, n_att = len(mlp_chunks), len(pieces)
    chunks = [(p.shape[0],) + p.shape[2:] for p in pieces]
    outs = [shape(part.shape), shape(h1_block.shape), shape((rows,) + small.shape, F32)]
    outs += [shape((count,) + c.shape) for c in mlp_chunks]
    outs += [shape((count,) + c) for c in chunks]
    scratch = [pltpu.VMEM((count - 1,) + c, BF16) for c in chunks]
    scratch += [pltpu.VMEM(c, BF16) for c in chunks]
    scratch += [pltpu.VMEM((count,) + small.shape, F32), dma(count - 1), dma(count - 1), dma(2)]
    scratch += [dma(n_mlp + n_att, 2), dma(n_mlp + n_att, count - 1), dma(n_mlp + n_att, count - 1)]
    scratch += [dma(n_att, count - 1), dma(n_att, count - 1)]
    scratch += reduce_scratch(rows, cols, height, width, True)
    scratch += reduce_scratch(rows, cols, height, width, False)
    outs = call(
        functools.partial(last_kernel, rows, cols, count, n_mlp, n_att),
        [part, part_out, h1_block, unit, small] + mlp_chunks + pieces,
        outs,
        scratch,
        3,
        "last_exchange",
    )
    return outs[0], outs[1], outs[2], outs[3:]


def swap_rows(value):
    return lax.ppermute(value, "row", [(0, 1), (1, 0)])


def half_of(value, index, axis):
    size = value.shape[axis] // 2
    return lax.dynamic_slice_in_dim(value, index * size, size, axis)


def in_order(row, own, other, axis):
    return jnp.where(
        row == 0,
        jnp.concatenate([own, other], axis),
        jnp.concatenate([other, own], axis),
    )


def whole_of_half(weight, row, cut, join):
    other = swap_rows(half_of(weight, 1 - row, cut))
    return in_order(row, half_of(weight, row, cut), other, join)


def unit_of(values):
    inverse = lax.rsqrt(jnp.mean(values * values, axis=1, keepdims=True) + NORM_EPS)
    return values * inverse, inverse


def norm_back(d_normed, gain, unit, inverse):
    scaled = d_normed * gain
    inner = jnp.sum(scaled * unit, axis=1, keepdims=True)
    return inverse * (scaled - unit * (inner / unit.shape[1]))


def layout(lengths, group_len):
    seq_ends = jnp.cumsum(lengths)
    token_place = jnp.arange(group_len, dtype=jnp.int32)
    seq_ids = jnp.sum((token_place[:, None] >= seq_ends[None, :]).astype(jnp.int32), axis=1)
    seq_starts = seq_ends - lengths
    onehot = (seq_ids[:, None] == jnp.arange(lengths.shape[0], dtype=jnp.int32)[None, :]).astype(
        jnp.int32
    )
    position = token_place - jnp.sum(onehot * seq_starts[None, :], axis=1)
    allowed = (seq_ids[:, None] == seq_ids[None, :]) & (
        token_place[None, :] <= token_place[:, None]
    )
    freqs = ROPE_THETA ** (-(jnp.arange(HEAD_DIM // 2, dtype=F32) * 2.0 / HEAD_DIM))
    angles = position.astype(F32)[:, None] * freqs[None, :]
    return (jnp.cos(angles), jnp.sin(angles), allowed)


def rotate(values, rot_cos, rot_sin):
    half_dim = HEAD_DIM // 2
    first, second = values[..., :half_dim], values[..., half_dim:]
    return jnp.concatenate(
        [first * rot_cos - second * rot_sin, second * rot_cos + first * rot_sin], axis=-1
    )


def to_heads(values):
    return [values[:, i : i + HEAD_DIM] for i in range(0, values.shape[1], HEAD_DIM)]


def in_chunks(grad):
    count = lax.axis_size("dp")
    grad = grad.astype(BF16)
    return grad.reshape(2, count, grad.shape[0] // (2 * count), grad.shape[1])


def from_chunks(summed, turned):
    halves = [summed[:, i].reshape(-1, summed.shape[3]).astype(F32) for i in range(2)]
    return jnp.concatenate([half.T for half in halves]) if turned else jnp.concatenate(halves, 1)


def on_device(
    tokens,
    seq_lengths,
    norm1_gain,
    w_query,
    w_key,
    w_value,
    b_query,
    b_key,
    b_value,
    w_out,
    norm2_gain,
    w_gate,
    w_up,
    w_down,
    cotangent,
):
    height, width = tokens.shape
    row, col = lax.axis_index("row"), lax.axis_index("col")
    rows, cols = lax.axis_size("row"), lax.axis_size("col")
    group_len = height * cols
    scale = HEAD_DIM ** (-0.5)

    def own_block(full):
        return lax.dynamic_slice(full, (col * height, row * width), (height, width))

    def joined_half(parts):
        return jnp.concatenate([half_of(part, row, 0) for part in parts])

    w_qkv_own = jnp.concatenate([half_of(w, row, 1) for w in (w_query, w_key, w_value)], 1)
    w_qkv_other = swap_rows(
        jnp.concatenate([half_of(w, 1 - row, 1) for w in (w_query, w_key, w_value)], 1)
    )
    w_qkv = in_order(row, w_qkv_own, w_qkv_other, 0)
    gains = jnp.stack([norm1_gain, norm2_gain])
    gains = in_order(row, gains, swap_rows(gains), 1)
    w_o = whole_of_half(w_out, row, 0, 1)

    token_full, cot_full = plane_gather([tokens, cotangent], 0)
    token_full, w_gate, w_up, w_down = lax.optimization_barrier((token_full, w_gate, w_up, w_down))
    w_g = whole_of_half(w_gate, row, 1, 0)
    w_u = whole_of_half(w_up, row, 1, 0)
    w_d = whole_of_half(w_down, row, 0, 1)
    resid = token_full.astype(F32)
    unit_one, inverse_one = unit_of(resid)
    normed_one = (unit_one * gains[0:1]).astype(BF16)
    qkv = dot_plain(normed_one, w_qkv) + joined_half((b_query, b_key, b_value))
    own_cols = qkv.shape[1] // 3
    rot_cos, rot_sin, allowed = layout(seq_lengths[0], group_len)
    q_heads = [rotate(h, rot_cos, rot_sin).astype(BF16) for h in to_heads(qkv[:, :own_cols])]
    k_heads = [
        rotate(h, rot_cos, rot_sin).astype(BF16) for h in to_heads(qkv[:, own_cols : 2 * own_cols])
    ]
    v_heads = [h.astype(BF16) for h in to_heads(qkv[:, 2 * own_cols :])]
    head_outs, head_probs = [], []
    for query, keys, values in zip(q_heads, k_heads, v_heads):
        scores = jnp.where(allowed, dot_right_t(query, keys) * scale, -1000000000.0)
        expo = jnp.exp(scores - jnp.max(scores, axis=-1, keepdims=True))
        probs = expo / jnp.sum(expo, axis=-1, keepdims=True)
        head_probs.append(probs)
        head_outs.append(dot_plain(probs.astype(BF16), values).astype(BF16))
    heads = jnp.concatenate(head_outs, 1)
    h1_full = plane_reduce(dot_plain(heads, w_o).astype(BF16), tokens)
    h1_full, late_cot = lax.optimization_barrier((h1_full, cot_full))
    unit_two, inverse_two = unit_of(h1_full.astype(F32))
    normed_two = (unit_two * gains[1:2]).astype(BF16)
    gate, upper = dot_plain(normed_two, w_g), dot_plain(normed_two, w_u)
    sigmoid_gate = jax.nn.sigmoid(gate)
    silu_gate = gate * sigmoid_gate
    hidden = (silu_gate * upper).astype(BF16)
    d_hidden = dot_right_t(late_cot, w_d).astype(BF16).astype(F32)
    d_gate = (d_hidden * upper * sigmoid_gate * (1.0 + gate * (1.0 - sigmoid_gate))).astype(BF16)
    d_upper = (d_hidden * silu_gate).astype(BF16)
    part = (dot_right_t(d_gate, w_g) + dot_right_t(d_upper, w_u)).astype(BF16)
    pieces = [dot_left_t(normed_two, d_gate), dot_left_t(normed_two, d_upper)]
    pieces.append(dot_left_t(cot_full, hidden))
    d_normed_two, mlp_chunks = mlp_back_reduce(part, [in_chunks(p) for p in pieces])
    d_normed_two = d_normed_two.astype(F32)
    d_h1 = norm_back(d_normed_two, gains[1:2], unit_two, inverse_two) + cot_full.astype(F32)
    own_half = row * width
    d_gain_two = jnp.sum(d_normed_two * unit_two, axis=0)
    d_gain_two = lax.dynamic_slice_in_dim(d_gain_two, own_half, width)

    d_branch = d_h1.astype(BF16)
    d_heads = dot_right_t(d_branch, w_o).astype(BF16)
    d_q, d_k, d_v = [], [], []
    for query, keys, values, probs, d_out in zip(
        q_heads, k_heads, v_heads, head_probs, to_heads(d_heads)
    ):
        d_v.append(dot_left_t(probs.astype(BF16), d_out))
        d_probs = dot_right_t(d_out, values)
        d_scores = (
            probs * (d_probs - jnp.sum(probs * d_probs, axis=-1, keepdims=True))
        ).astype(BF16)
        d_q.append(rotate(dot_plain(d_scores, keys) * scale, rot_cos, -rot_sin))
        d_k.append(rotate(dot_left_t(d_scores, query) * scale, rot_cos, -rot_sin))
    d_qkv = jnp.concatenate(d_q + d_k + d_v, 1).astype(BF16)
    part = dot_right_t(d_qkv, w_qkv).astype(BF16)
    pieces = [
        in_chunks(dot_left_t(normed_one, d_qkv[:, i * own_cols : (i + 1) * own_cols]))
        for i in range(3)
    ]
    pieces.append(in_chunks(dot_left_t(d_branch, heads)))
    d_bias = jnp.sum(d_qkv.astype(F32), axis=0)
    small = jnp.zeros((8, width), F32)
    small = small.at[1].set(d_gain_two)
    small = small.at[2:5, :own_cols].set(d_bias.reshape(3, own_cols))
    unit_own = lax.dynamic_slice_in_dim(unit_one, own_half, width, 1)
    part_out = dot_plain(hidden, w_d).astype(BF16)
    d_normed_one, layer_out, small, summed = last_exchange(
        part, part_out, own_block(h1_full), unit_own, small, mlp_chunks, pieces
    )
    d_tokens = norm_back(d_normed_one.astype(F32), gains[0:1], unit_one, inverse_one) + d_h1
    d_tokens = own_block(d_tokens.astype(BF16))
    own_small = lax.dynamic_index_in_dim(small, row, 0, keepdims=False)
    bias_sum = [small[:, 2 + i, :own_cols].reshape(-1) for i in range(3)]
    summed = [from_chunks(item, i in (2, 6)) for i, item in enumerate(summed)]
    return (
        layer_out,
        d_tokens,
        own_small[0],
        summed[3],
        summed[4],
        summed[5],
        bias_sum[0],
        bias_sum[1],
        bias_sum[2],
        summed[6],
        own_small[1],
        summed[0],
        summed[1],
        summed[2],
    )


def solution(mesh):
    block = P(("dp", "col"), "row")
    down, across = P("row", "col"), P("col", "row")
    return jax.shard_map(
        on_device,
        mesh=mesh,
        in_specs=(
            block,
            P("dp", None),
            P("row"),
            down,
            down,
            down,
            P("col"),
            P("col"),
            P("col"),
            across,
            P("row"),
            down,
            down,
            across,
            block,
        ),
        out_specs=(
            block,
            block,
            P("row"),
            down,
            down,
            down,
            P("col"),
            P("col"),
            P("col"),
            across,
            P("row"),
            down,
            down,
            across,
        ),
        check_vma=False,
    )
```
